32 devices in a mesh: stack: 2 (over y), acq: 4 (over z), lines: 4 (over x, core).
Axes of the slice: x: 2, y: 2, z: 4, core: 2. Of those that a mesh axis runs over, the one named last changes fastest.
Arguments:
- returned_radar_signal_data: bfloat16 [8, 2, 512, 4096], P(('stack', 'acq'), None, 'lines'), parts along dimension 0, may hold values from -6 to 6
- slant_replica_filter_response: float32 [8, 2, 4096], P(('stack', 'acq')), parts along dimension 0, may hold values from -6 to 6
- along_track_sharpening_slope: float32 [8, 4096], P(('stack', 'acq'), 'lines'), parts along dimension 0, may hold values from 0.25 to 1
- motion_shift_centroid_hz: float32 [8, 4096], P(('stack', 'acq'), 'lines'), parts along dimension 0, may hold values from -0.2 to 0.2
- valid_along_track_rows: int32 [8], P(('stack', 'acq')), parts along dimension 0, may hold values from 256 to 512, as said below
- reference_index: int32 [2], P('stack'), parts along dimension 0, may hold values from 0 to 3
- patch_offsets: int32 [8, 2, 4, 32], P(('stack', 'acq'), None, None, 'lines'), parts along dimension 0, may hold values from -64 to 64
Outputs:
- correlation: float32 [8, 2, 256, 2048], P(('stack', 'acq'), None, None, 'lines'), parts along dimension 0
The draws below stay inside these ranges and needn't reach their ends.
There are 2 independent parts, one for each index of `stack`. The reference program is written for one: setup_inputs(seed, part) draws one part's arguments, and reference() takes and returns one part's arrays. A program takes and returns all parts, laid end to end along the dimension named above; each array names one. Nothing has to cross between parts.
Inputs may be any that keep to these rules, and one draw needn't show every extreme that they name: `valid_along_track_rows`: some acquisition has all 512 lines valid and some exactly half of them.
All inputs are finite; a program needn't handle non-finite values.
Results may differ from the reference program's by a relative error of at most 0.0053.
Values may be sent and summed in bfloat16 or wider, within the bound.
No kernel may reach another device: no remote copies, remote signals or barrier semaphores. Data moves between devices by JAX's collectives and lax.ppermute only.
A program may use at most 64 MiB of HBM per device.

```python
import math
import jax
import jax.numpy as jnp
from jax import lax

NA = 512
NR = 4096
PATCH = 64
ACQ = 4


def draw_valid_along_track_rows(key, part):
    counts = jax.random.randint(jax.random.fold_in(key, 11), (ACQ,), NA // 2, NA + 1)
    order = jax.random.permutation(jax.random.fold_in(key, 12), ACQ)
    counts = jnp.where(order == 0, NA, counts)
    counts = jnp.where(order == 1, NA // 2, counts)
    return counts.astype(jnp.int32)


def set_ends(array, own_key, least, top_value):
    longest = array.shape.index(max(array.shape))
    spots = []
    for shift in (0, 1):
        where = [jax.random.randint(jax.random.fold_in(own_key, axis), (), 0, length) for axis, length in enumerate(array.shape)]
        where[longest] = (where[longest] + shift) % array.shape[longest]
        spots.append(tuple(where))
    return array.at[spots[0]].set(least).at[spots[1]].set(top_value)


def block_scale(own_key, extent, pieces, least, high):
    gain, own = 1.0, jax.random.fold_in(own_key, 6)
    for axis_at, shards_of in pieces:
        draws = jnp.exp(jax.random.uniform(jax.random.fold_in(own, axis_at), (shards_of,), jnp.float32, least / len(pieces), high / len(pieces)))
        gain = gain * jnp.repeat(draws, extent[axis_at] // shards_of).reshape([-1 if axis == axis_at else 1 for axis in range(len(extent))])
    return gain


def bell_draw(own_key, shape, deviation, reach, shards=(), kind=jnp.bfloat16):
    level = block_scale(own_key, shape, shards, -0.22, 0.18) if shards else 1.0
    result = jax.random.normal(own_key, shape, jnp.float32) * deviation * level
    return jnp.minimum(jnp.maximum(result, -reach), reach).astype(kind)


def setup_inputs(seed: int = 0, part: int = 0) -> dict:
    key_list = jax.random.split(jax.random.key(seed), 8)
    own_keys = jax.random.split(jax.random.fold_in(key_list[7], part), 8)
    returned_radar_signal_data = bell_draw(own_keys[0], (ACQ, 2, NA, NR), 0.7, 6.0, ((0, 4), (2, 4)))
    slant_replica_filter_response = bell_draw(own_keys[1], (ACQ, 2, NR), 0.7, 6.0, ((0, 4),), jnp.float32)
    along_track_sharpening_slope = jnp.clip(jnp.exp(math.log(1.0) - 1.3862944 * jax.random.uniform(own_keys[2], (ACQ, NR), jnp.float32) ** block_scale(own_keys[2], (ACQ, NR), ((0, 4), (1, 4)), -0.2, 0.2)), 0.25, 1.0)
    motion_shift_centroid_hz = jnp.clip(jax.random.uniform(own_keys[3], (ACQ, NR), jnp.float32, -0.2, 0.2) * block_scale(own_keys[3], (ACQ, NR), ((0, 4), (1, 4)), -0.4, 0.0), -0.2, 0.2)
    valid_along_track_rows = draw_valid_along_track_rows(jax.random.fold_in(jax.random.fold_in(key_list[7], part), 71), part)
    reference_index = jax.random.randint(own_keys[5], (1,), 0, ACQ).astype(jnp.int32)
    patch_offsets = set_ends(jax.random.randint(own_keys[6], (ACQ, 2, NA // (2 * PATCH), NR // (2 * PATCH)), -PATCH, PATCH + 1), jax.random.fold_in(own_keys[6], 1), -PATCH, PATCH).astype(jnp.int32)
    return {"returned_radar_signal_data": returned_radar_signal_data, "slant_replica_filter_response": slant_replica_filter_response, "along_track_sharpening_slope": along_track_sharpening_slope, "motion_shift_centroid_hz": motion_shift_centroid_hz, "valid_along_track_rows": valid_along_track_rows, "reference_index": reference_index, "patch_offsets": patch_offsets}


eps = 1e-06

def sharpen_one_pulse_group(vectorized_inputs):
    raw_one, filter_one, rate_one, centre_one, valid_one = vectorized_inputs
    line_index = jnp.arange(NA, dtype=jnp.int32)[:, None]
    keep_mask = (line_index < valid_one).astype(jnp.float32)
    echo = lax.complex(raw_one[0].astype(jnp.float32) * keep_mask, raw_one[1].astype(jnp.float32) * keep_mask)
    spectrum = jnp.fft.fft(echo, axis=1) * lax.complex(filter_one[0], filter_one[1])[None, :]
    compressed = jnp.fft.ifft(spectrum, axis=1)
    real_part = lax.optimization_barrier(jnp.real(compressed).astype(jnp.bfloat16)).astype(jnp.float32)
    imaginary = lax.optimization_barrier(jnp.imag(compressed).astype(jnp.bfloat16)).astype(jnp.float32)
    along = jnp.fft.fft(lax.complex(real_part, imaginary), axis=0)
    freq_index = jnp.arange(NA, dtype=jnp.int32)
    signed_freq = jnp.where(freq_index >= NA // 2, freq_index - NA, freq_index).astype(jnp.float32) / NA
    offset_freq = signed_freq[:, None] - centre_one[None, :]
    phase_angle = math.pi * NA / 4.0 * rate_one[None, :] * offset_freq * offset_freq
    along = along * lax.complex(jnp.cos(phase_angle), jnp.sin(phase_angle))
    focused = jnp.fft.ifft(along, axis=0)
    return jnp.stack([jnp.real(focused), jnp.imag(focused)]).astype(jnp.bfloat16)

def reference(returned_radar_signal_data, slant_replica_filter_response, along_track_sharpening_slope, motion_shift_centroid_hz, valid_along_track_rows, reference_index, patch_offsets):
    sharpened_acquisition_pictures = lax.map(sharpen_one_pulse_group, (returned_radar_signal_data, slant_replica_filter_response, along_track_sharpening_slope, motion_shift_centroid_hz, valid_along_track_rows))
    primary_image = sharpened_acquisition_pictures[reference_index[0]].astype(jnp.float32)
    row_blocks = NA // (2 * PATCH)
    col_blocks = NR // (2 * PATCH)
    half = PATCH // 2
    blocks = primary_image.reshape(2, row_blocks, 2 * PATCH, col_blocks, 2 * PATCH)
    blocks = blocks[:, :, half:half + PATCH, :, half:half + PATCH]
    blocks = blocks.transpose(1, 3, 0, 2, 4).reshape(row_blocks * col_blocks, 2, PATCH, PATCH)
    primary_stack = lax.complex(blocks[:, 0], blocks[:, 1])
    primary_power = lax.optimization_barrier(jnp.mean(blocks[:, 0] * blocks[:, 0] + blocks[:, 1] * blocks[:, 1], axis=(1, 2)))
    primary_spectrum = jnp.fft.fft2(primary_stack)
    block_row = lax.broadcasted_iota(jnp.int32, (row_blocks, col_blocks), 0)
    block_col = lax.broadcasted_iota(jnp.int32, (row_blocks, col_blocks), 1)

    def correlate(vectorized_inputs):
        image, offsets = vectorized_inputs
        padded = jnp.pad(image.astype(jnp.float32), ((0, 0), (half, half), (half, half)))
        row_start = (2 * PATCH * block_row + PATCH + offsets[0]).reshape(-1)
        col_start = (2 * PATCH * block_col + PATCH + offsets[1]).reshape(-1)

        def window(start_row, start_col):
            zero = jnp.zeros((), jnp.int32)
            return lax.dynamic_slice(padded, (zero, start_row, start_col), (2, PATCH, PATCH))
        second_stack = jax.vmap(window)(row_start, col_start)
        second_power = lax.optimization_barrier(jnp.mean(second_stack[:, 0] * second_stack[:, 0] + second_stack[:, 1] * second_stack[:, 1], axis=(1, 2)))
        second_spectrum = jnp.fft.fft2(lax.complex(second_stack[:, 0], second_stack[:, 1]))
        surface = jnp.fft.ifft2(primary_spectrum * jnp.conj(second_spectrum))
        scale = 1.0 / (PATCH * jnp.sqrt(primary_power + eps) * jnp.sqrt(second_power + eps))
        surface = surface * scale[:, None, None]
        stacked = jnp.stack([jnp.real(surface), jnp.imag(surface)]).astype(jnp.float32)
        stacked = stacked.reshape(2, row_blocks, col_blocks, PATCH, PATCH).transpose(0, 1, 3, 2, 4)
        return stacked.reshape(2, row_blocks * PATCH, col_blocks * PATCH)
    return lax.map(correlate, (sharpened_acquisition_pictures, patch_offsets))
```

```python
import functools
import math

import jax
import jax.numpy as jnp
import ml_dtypes
import numpy as np
from jax import lax
from jax.experimental import pallas as pl
from jax.experimental.pallas import tpu as pltpu
from jax.sharding import PartitionSpec as P

PATCH = 64
LANES = 128
HALF = PATCH // 2
EPS = 1e-06
F32 = jnp.float32
BF16 = jnp.bfloat16
VMEM_BYTES = 56 * 1024 * 1024

SIN_POLY = (3.141582022139052, -5.167142795074894, 2.541899011376644, -0.5546361478584824)
COS_POLY = (0.9999933027022169, -4.9339382503784215, 4.041285686469419, -1.2221312612719153)


def split_np(matrix):
    high = matrix.astype(ml_dtypes.bfloat16)
    low = (matrix - high.astype(np.float64)).astype(ml_dtypes.bfloat16)
    return high, low


def angle_np(rows, cols, period):
    return 2.0 * np.pi * ((np.asarray(rows)[:, None] * np.asarray(cols)[None, :]) % period) / period


def right_matrix(theta, sign, scale=1.0):
    cos, sin = np.cos(theta) * scale, sign * np.sin(theta) * scale
    return split_np(np.block([[cos, sin], [-sin, cos]]))


def left_matrix(theta, sign, scale=1.0):
    cos, sin = np.cos(theta) * scale, sign * np.sin(theta) * scale
    return split_np(np.block([[cos, -sin], [sin, cos]]))


def split(value):
    high = value.astype(BF16)
    low = (value - high.astype(F32)).astype(BF16)
    return high, low


def dot(lhs, rhs):
    return jnp.dot(lhs, rhs, preferred_element_type=F32)


def fft_list(re, im, sign):
    size = len(re)
    if size == 1:
        return re, im
    if size == 2:
        return [re[0] + re[1], re[0] - re[1]], [im[0] + im[1], im[0] - im[1]]
    even_re, even_im = fft_list(re[0::2], im[0::2], sign)
    odd_re, odd_im = fft_list(re[1::2], im[1::2], sign)
    half = size // 2
    out_re, out_im = [None] * size, [None] * size
    root = math.sqrt(0.5)
    for k in range(half):
        a, b = odd_re[k], odd_im[k]
        if k == 0:
            t_re, t_im = a, b
        elif 4 * k == size:
            t_re, t_im = (b, -a) if sign < 0 else (-b, a)
        elif 8 * k == size:
            t_re, t_im = ((a + b) * root, (b - a) * root) if sign < 0 else ((a - b) * root, (a + b) * root)
        elif 8 * k == 3 * size:
            t_re, t_im = ((b - a) * root, (a + b) * -root) if sign < 0 else ((a + b) * -root, (a - b) * root)
        else:
            cos = math.cos(2.0 * math.pi * k / size)
            sin = sign * math.sin(2.0 * math.pi * k / size)
            t_re, t_im = a * cos - b * sin, a * sin + b * cos
        if 4 * k == size:
            if sign < 0:
                out_re[k], out_re[k + half] = even_re[k] + b, even_re[k] - b
                out_im[k], out_im[k + half] = even_im[k] - a, even_im[k] + a
            else:
                out_re[k], out_re[k + half] = even_re[k] - b, even_re[k] + b
                out_im[k], out_im[k + half] = even_im[k] + a, even_im[k] - a
            continue
        out_re[k], out_re[k + half] = even_re[k] + t_re, even_re[k] - t_re
        out_im[k], out_im[k + half] = even_im[k] + t_im, even_im[k] - t_im
    return out_re, out_im


def three_pass(lhs, high, low):
    lhs_high, lhs_low = lhs
    return dot(lhs_high, high) + dot(lhs_low, high) + dot(lhs_high, low)


def range_kernel(info, x_ref, filt_ref, twf_ref, twi_ref, mfh, mfl, mih, mil, *rest, devices, sub):
    outs, (in_scr, out_scr) = rest[: 2 * devices], rest[2 * devices :]
    inner_refs, outer_refs = outs[:devices], outs[devices:]
    rows, length = x_ref.shape[1], x_ref.shape[2]
    count = length // LANES
    per = count // devices
    me, valid = info[0], info[1]
    first = (me * pl.num_programs(0) + pl.program_id(0)) * rows
    lane = lax.broadcasted_iota(jnp.int32, (sub, LANES), 1)
    for block in range(rows // sub):
        span = slice(block * sub, (block + 1) * sub)
        line = first + block * sub + lax.broadcasted_iota(jnp.int32, (sub, LANES), 0)
        keep = line < valid
        re, im = [], []
        for a in range(count):
            at = slice(a * LANES, (a + 1) * LANES)
            re.append(jnp.where(keep, x_ref[0, span, at].astype(F32), 0.0))
            im.append(jnp.where(keep, x_ref[1, span, at].astype(F32), 0.0))
        re, im = fft_list(re, im, -1)
        high, low = [], []
        for c in range(count):
            cos, sin = twf_ref[0, c : c + 1, :], twf_ref[1, c : c + 1, :]
            h_re, l_re = split(re[c] * cos - im[c] * sin)
            h_im, l_im = split(re[c] * sin + im[c] * cos)
            high.append(jnp.concatenate([h_re, h_im], axis=1))
            low.append(jnp.concatenate([l_re, l_im], axis=1))
        spectrum = three_pass((jnp.concatenate(high, 0), jnp.concatenate(low, 0)), mfh[...], mfl[...])
        high, low = [], []
        for c in range(count):
            at = slice(c * sub, (c + 1) * sub)
            a, b = spectrum[at, :LANES], spectrum[at, LANES:]
            cos, sin = filt_ref[0, c : c + 1, :], filt_ref[1, c : c + 1, :]
            h_re, l_re = split(a * cos - b * sin)
            h_im, l_im = split(a * sin + b * cos)
            high.append(jnp.concatenate([h_re, h_im], axis=1))
            low.append(jnp.concatenate([l_re, l_im], axis=1))
        pulse = three_pass((jnp.concatenate(high, 0), jnp.concatenate(low, 0)), mih[...], mil[...])
        re, im = [], []
        for c in range(count):
            at = slice(c * sub, (c + 1) * sub)
            a, b = pulse[at, :LANES], pulse[at, LANES:]
            cos, sin = twi_ref[0, c : c + 1, :], twi_ref[1, c : c + 1, :]
            re.append(a * cos - b * sin)
            im.append(a * sin + b * cos)
        parts = fft_list(re, im, 1)
        zero = jnp.zeros((sub, LANES), F32)
        for part in range(2):
            y = list(parts[part])
            group = [jnp.where(lane < 96, y[a - 1] if a else zero, y[a] if a < count else zero) for a in range(count + 1)]
            group.append(zero)
            for u in range(count // 2):
                in_scr[u, part, span, :] = jnp.where(
                    lane < 64, y[2 * u], pltpu.roll(y[2 * u + 1], 64, 1)
                ).astype(BF16)
            for u in range(count // 2 + 1):
                out_scr[u, part, span, :] = jnp.where(
                    lane < 64, pltpu.roll(group[2 * u], 64, 1), group[2 * u + 1]
                ).astype(BF16)
    for k in range(devices):
        base = (me ^ k) * (per // 2)
        for t in range(per // 2):
            inner_refs[k][:, :, t * LANES : (t + 1) * LANES] = in_scr[base + t]
        for t in range(per // 2 + 1):
            outer_refs[k][:, :, t * LANES : (t + 1) * LANES] = out_scr[base + t]


def compress(echo, filt, me, valid, devices):
    _, rows, length = echo.shape
    count = length // LANES
    per = count // devices
    step = min(32, rows)
    sub = 16
    natural = np.arange(LANES)
    turned = (natural + HALF) % LANES
    twf = -angle_np(np.arange(count), natural, length)
    twi = angle_np(np.arange(count), turned, length)
    twf = jnp.asarray(np.stack([np.cos(twf), np.sin(twf)]), F32)
    twi = jnp.asarray(np.stack([np.cos(twi), np.sin(twi)]), F32)
    mats = right_matrix(angle_np(natural, natural, LANES), -1) + right_matrix(
        angle_np(natural, turned, LANES), 1, 1.0 / length
    )
    widths = [per // 2 * LANES] * devices + [(per // 2 + 1) * LANES] * devices
    whole2 = pl.BlockSpec((2 * LANES, 2 * LANES), lambda i, _: (0, 0))
    whole3 = pl.BlockSpec((2, count, LANES), lambda i, _: (0, 0, 0))
    outs = pl.pallas_call(
        functools.partial(range_kernel, devices=devices, sub=sub),
        grid_spec=pltpu.PrefetchScalarGridSpec(
            num_scalar_prefetch=1,
            grid=(rows // step,),
            in_specs=[pl.BlockSpec((2, step, length), lambda i, _: (0, i, 0)), whole3, whole3, whole3]
            + [whole2] * 4,
            out_specs=[pl.BlockSpec((2, step, w), lambda i, _: (0, i, 0)) for w in widths],
            scratch_shapes=[
                pltpu.VMEM((count // 2, 2, step, LANES), BF16),
                pltpu.VMEM((count // 2 + 1, 2, step, LANES), BF16),
            ],
        ),
        out_shape=[jax.ShapeDtypeStruct((2, rows, w), BF16) for w in widths],
        compiler_params=pltpu.CompilerParams(vmem_limit_bytes=VMEM_BYTES),
        name="range_compress",
    )(
        jnp.stack([me, valid]).astype(jnp.int32),
        echo,
        filt.reshape(2, LANES, count).transpose(0, 2, 1),
        twf,
        twi,
        *[jnp.asarray(m) for m in mats],
    )
    return outs[:devices], outs[devices:]


def turn(turns):
    x = turns - jnp.round(turns)
    z = x * x
    sin = x * (SIN_POLY[0] + z * (SIN_POLY[1] + z * (SIN_POLY[2] + z * SIN_POLY[3])))
    cos = COS_POLY[0] + z * (COS_POLY[1] + z * (COS_POLY[2] + z * COS_POLY[3]))
    return 1.0 - 2.0 * (sin * sin), 2.0 * (sin * cos)


def focus_tile(scr, col, width, slope, centre, af_ref, ai_ref):
    lines = scr.shape[1]
    radix = lines // LANES
    at = slice(col, col + width)
    re = [scr[0, s * LANES : (s + 1) * LANES, at].astype(F32) for s in range(radix)]
    im = [scr[1, s * LANES : (s + 1) * LANES, at].astype(F32) for s in range(radix)]
    re, im = fft_list(re, im, -1)
    d = lax.broadcasted_iota(jnp.int32, (LANES, width), 0)
    back_re, back_im = [], []
    rate = slope * (lines / 8.0)
    for c in range(radix):
        high, low = split(jnp.concatenate([re[c], im[c]], axis=0))
        rhs = jnp.concatenate([high, low, high], axis=0)
        freq = dot(af_ref[c], rhs)
        k = c + radix * d
        u = jnp.where(k >= lines // 2, k - lines, k).astype(F32) * (1.0 / lines)
        w = u - centre
        cos, sin = turn(rate * w * w)
        a, b = freq[:LANES], freq[LANES:]
        high, low = split(jnp.concatenate([a * cos - b * sin, a * sin + b * cos], axis=0))
        rhs = jnp.concatenate([high, low, high], axis=0)
        back = dot(ai_ref[c], rhs)
        back_re.append(back[:LANES])
        back_im.append(back[LANES:])
    return fft_list(back_re, back_im, 1)


def azimuth_matrices(lines):
    radix = lines // LANES
    t = np.arange(LANES)
    forward, inverse = [], []
    for c in range(radix):
        k = c + radix * t
        high, low = left_matrix(angle_np(k, t, lines), -1)
        forward.append(np.concatenate([high, high, low], axis=1))
        high, low = left_matrix(angle_np(t, k, lines), 1, 1.0 / lines)
        inverse.append(np.concatenate([high, high, low], axis=1))
    return jnp.asarray(np.stack(forward)), jnp.asarray(np.stack(inverse))


def gather_lines(info, blocks, scr):
    rows = blocks[0].shape[1]
    for k, block in enumerate(blocks):
        start = pl.multiple_of((info[0] ^ k) * rows, rows)
        scr[:, pl.ds(start, rows), :] = block[...]


def inner_kernel(info, *rest, devices, parts):
    blocks, rest = rest[:devices], rest[devices:]
    slope_ref, centre_ref, af_ref, ai_ref, out_ref = rest[:5]
    p_refs, (scr, p_scr) = rest[5 : 5 + parts], rest[5 + parts :]
    gather_lines(info, blocks, scr)
    width = out_ref.shape[2]
    lane = lax.broadcasted_iota(jnp.int32, (1, LANES), 1)

    def packed(ref):
        tiles = []
        for t in range(width // LANES):
            a = pltpu.roll(ref[:, 2 * t * LANES : (2 * t + 1) * LANES], 96, 1)
            b = pltpu.roll(ref[:, (2 * t + 1) * LANES : (2 * t + 2) * LANES], 32, 1)
            tiles.append(jnp.where(lane < 64, a, b))
        return jnp.concatenate(tiles, axis=1)

    re, im = focus_tile(scr, 0, width, packed(slope_ref), packed(centre_ref), af_ref, ai_ref)
    for part, value in enumerate((re, im)):
        for s in range(len(value)):
            image = value[s].astype(BF16)
            out_ref[part, s * LANES : (s + 1) * LANES, :] = image
            p_scr[part, s * PATCH : (s + 1) * PATCH, :] = image[HALF : HALF + PATCH]
    share = p_scr.shape[1] // parts
    for k in range(parts):
        start = pl.multiple_of((info[1] ^ k) * share, share)
        p_refs[k][...] = p_scr[:, pl.ds(start, share), :]


def focus_inner(blocks, slope, centre, matrices, me, me_acq, parts):
    devices = len(blocks)
    _, rows, cols = blocks[0].shape
    lines = rows * devices
    tile = 2 * LANES if cols % (2 * LANES) == 0 else LANES
    prows = lines // 2
    shape = (lines // LANES, 2 * LANES, 6 * LANES)
    return pl.pallas_call(
        functools.partial(inner_kernel, devices=devices, parts=parts),
        grid_spec=pltpu.PrefetchScalarGridSpec(
            num_scalar_prefetch=1,
            grid=(cols // tile,),
            in_specs=[pl.BlockSpec((2, rows, tile), lambda i, _: (0, 0, i))] * devices
            + [pl.BlockSpec((1, 2 * tile), lambda i, _: (0, i))] * 2
            + [pl.BlockSpec(shape, lambda i, _: (0, 0, 0))] * 2,
            out_specs=[pl.BlockSpec((2, lines, tile), lambda i, _: (0, 0, i))]
            + [pl.BlockSpec((2, prows // parts, tile), lambda i, _: (0, 0, i))] * parts,
            scratch_shapes=[pltpu.VMEM((2, lines, tile), BF16), pltpu.VMEM((2, prows, tile), BF16)],
        ),
        out_shape=[jax.ShapeDtypeStruct((2, lines, cols), BF16)]
        + [jax.ShapeDtypeStruct((2, prows // parts, cols), BF16)] * parts,
        compiler_params=pltpu.CompilerParams(vmem_limit_bytes=VMEM_BYTES),
        name="focus_inner",
    )(jnp.stack([me, me_acq]).astype(jnp.int32), *blocks, slope, centre, *matrices)


def patch_matrices():
    n = np.arange(PATCH)
    theta = angle_np(n, n, PATCH)

    def lanes(sign):
        cos = np.kron(np.eye(2), np.cos(theta))
        sin = sign * np.kron(np.eye(2), np.sin(theta))
        return np.stack(split_np(np.block([[cos, sin], [-sin, cos]])))

    high, low = split_np(np.concatenate([np.cos(theta), np.sin(theta)], axis=0))
    column = np.concatenate([high, high, low], axis=1)
    return jnp.asarray(lanes(-1)), jnp.asarray(lanes(1)), jnp.asarray(column)


def columns(value, column_ref, sign):
    high, low = split(value)
    both = dot(column_ref[...], jnp.concatenate([high, low, high], axis=0))
    c_re, c_im = both[:PATCH, :LANES], both[:PATCH, LANES:]
    s_re, s_im = both[PATCH:, :LANES], both[PATCH:, LANES:]
    if sign < 0:
        return c_re + s_im, c_im - s_re
    return c_re - s_im, c_im + s_re


def power(re, im):
    lane = lax.broadcasted_iota(jnp.int32, (1, LANES), 1)
    total = jnp.sum(re * re + im * im, axis=0, keepdims=True)
    left = jnp.sum(jnp.where(lane < PATCH, total, 0.0), axis=1, keepdims=True)
    right = jnp.sum(jnp.where(lane < PATCH, 0.0, total), axis=1, keepdims=True)
    return jnp.where(lane < PATCH, left, right) * (1.0 / (PATCH * PATCH))


def outer_kernel(info, offsets, *rest, devices):
    blocks, rest = rest[:devices], rest[devices:]
    inner_ref, slope_ref, centre_ref, af_ref, ai_ref, lane_ref, column_ref = rest[:7]
    spec_ref, gain_ref, scr, image, windows = rest[7:]
    gather_lines(info, blocks, scr)
    lines, width = scr.shape[1], scr.shape[2]
    lane = lax.broadcasted_iota(jnp.int32, (1, LANES), 1)
    pairs = width // LANES - 1

    def group(ref, a):
        before = ref[:, a * LANES : (a + 1) * LANES]
        after = ref[:, (a + 1) * LANES : (a + 2) * LANES]
        return jnp.where(lane < 96, pltpu.roll(before, 96, 1), pltpu.roll(after, 96, 1))

    def packed(ref, u):
        left = pltpu.roll(group(ref, 2 * u), 64, 1)
        if u == pairs:
            return jnp.where(lane < 64, left, 0.0)
        return jnp.where(lane < 64, left, group(ref, 2 * u + 1))

    edge = jnp.zeros((HALF, image.shape[2]), F32)
    for part in range(2):
        image[part, :HALF, :] = edge
        image[part, HALF + lines : 2 * HALF + lines, :] = edge
    for u in range(pairs + 1):
        re, im = focus_tile(scr, u * LANES, LANES, packed(slope_ref, u), packed(centre_ref, u), af_ref, ai_ref)
        for part, value in enumerate((re, im)):
            for s in range(len(value)):
                at = slice(HALF + s * LANES, HALF + (s + 1) * LANES)
                fresh = value[s].astype(BF16).astype(F32)
                if u == pairs:
                    image[part, at, 2 * u * LANES : (2 * u + 1) * LANES] = fresh
                    continue
                known = inner_ref[part, s * LANES : (s + 1) * LANES, u * LANES : (u + 1) * LANES].astype(F32)
                image[part, at, 2 * u * LANES : (2 * u + 1) * LANES] = jnp.where(
                    lane < 64, fresh, pltpu.roll(known, 64, 1)
                )
                image[part, at, (2 * u + 1) * LANES : (2 * u + 2) * LANES] = jnp.where(
                    lane < 64, pltpu.roll(fresh, 64, 1), known
                )
    row_blocks = lines // (2 * PATCH)
    wide = lax.broadcasted_iota(jnp.int32, (PATCH + 8, LANES), 1)
    for i in range(row_blocks):
        for u in range(pairs):
            found = [[], []]
            for side in range(2):
                j = 2 * u + side
                start = 2 * PATCH * i + PATCH + offsets[0, i, j]
                shift = PATCH + offsets[1, i, j]
                back = jnp.bitwise_and(2 * LANES - shift + side * PATCH, LANES - 1)
                base = pl.multiple_of(lax.shift_left(lax.shift_right_logical(start, 3), 3), 8)
                up = PATCH + 8 - jnp.bitwise_and(start, 7)
                for part in range(2):
                    left = image[part, pl.ds(base, PATCH + 8), j * LANES : (j + 1) * LANES]
                    right = image[part, pl.ds(base, PATCH + 8), (j + 1) * LANES : (j + 2) * LANES]
                    turned = pltpu.roll(jnp.where(wide >= shift, left, right), back, 1)
                    found[part].append(pltpu.roll(turned, up, 0)[:PATCH])
            re = jnp.where(lane < PATCH, found[0][0], found[0][1])
            im = jnp.where(lane < PATCH, found[1][0], found[1][1])
            at = i * pairs + u
            gain_ref[at] = jnp.broadcast_to(lax.rsqrt(power(re, im) + EPS), gain_ref.shape[1:])
            windows[at * PATCH : (at + 1) * PATCH, :] = jnp.concatenate([re, im], axis=1).astype(BF16)
    mixed = dot(windows[...], lane_ref[0]) + dot(windows[...], lane_ref[1])
    for at in range(row_blocks * pairs):
        re, im = columns(mixed[at * PATCH : (at + 1) * PATCH], column_ref, -1)
        spec_ref[0, at] = re
        spec_ref[1, at] = im


def focus_outer(blocks, inner, slope, centre, matrices, patch, me, offsets):
    devices = len(blocks)
    _, rows, cols = blocks[0].shape
    lines = rows * devices
    pairs = cols // LANES - 1
    groups = lines // (2 * PATCH) * pairs
    vmem = pl.BlockSpec(memory_space=pltpu.VMEM)
    smem = pl.BlockSpec(memory_space=pltpu.SMEM)
    return pl.pallas_call(
        functools.partial(outer_kernel, devices=devices),
        in_specs=[smem, smem] + [vmem] * (devices + 7),
        out_specs=[vmem, vmem],
        out_shape=[
            jax.ShapeDtypeStruct((2, groups, PATCH, LANES), F32),
            jax.ShapeDtypeStruct((groups, 8, LANES), F32),
        ],
        scratch_shapes=[
            pltpu.VMEM((2, lines, cols), BF16),
            pltpu.VMEM((2, lines + 2 * HALF + 8, (2 * pairs + 1) * LANES), F32),
            pltpu.VMEM((groups * PATCH, 2 * LANES), BF16),
        ],
        compiler_params=pltpu.CompilerParams(vmem_limit_bytes=VMEM_BYTES),
        name="focus_outer",
    )(me.reshape(1).astype(jnp.int32), offsets, *blocks, inner, slope, centre, *matrices, patch[0], patch[2])


def correlate_kernel(info, *rest, parts):
    shares, rest = rest[:parts], rest[parts:]
    spec_ref, gain_ref, forward_ref, inverse_ref, column_ref, out_ref, p_scr = rest
    share = shares[0].shape[1]
    for k in range(parts):
        start = pl.multiple_of((info[0] ^ k) * share, share)
        p_scr[:, pl.ds(start, share), :] = shares[k][...]
    prows, cols = p_scr.shape[1], p_scr.shape[2]
    pairs = cols // LANES
    groups = prows // PATCH * pairs
    first = []
    for at in range(groups):
        i, u = divmod(at, pairs)
        rows, lanes = slice(i * PATCH, (i + 1) * PATCH), slice(u * LANES, (u + 1) * LANES)
        first.append(jnp.concatenate([p_scr[0, rows, lanes], p_scr[1, rows, lanes]], axis=1))
    stack = jnp.concatenate(first, axis=0)
    mixed = dot(stack, forward_ref[0]) + dot(stack, forward_ref[1])
    middle, gains = [], []
    for at in range(groups):
        i, u = divmod(at, pairs)
        p = first[at].astype(F32)
        gain = lax.rsqrt(power(p[:, :LANES], p[:, LANES:]) + EPS) * gain_ref[at][:1]
        gains.append(gain * (1.0 / PATCH**3))
        p_re, p_im = columns(mixed[at * PATCH : (at + 1) * PATCH], column_ref, -1)
        s_re, s_im = spec_ref[0, at], spec_ref[1, at]
        cross = jnp.concatenate([p_re * s_re + p_im * s_im, p_im * s_re - p_re * s_im], axis=1)
        re, im = columns(cross, column_ref, 1)
        middle.append(jnp.concatenate([re, im], axis=1))
    surface = three_pass(split(jnp.concatenate(middle, axis=0)), inverse_ref[0], inverse_ref[1])
    for at in range(groups):
        i, u = divmod(at, pairs)
        block = surface[at * PATCH : (at + 1) * PATCH]
        rows, lanes = slice(i * PATCH, (i + 1) * PATCH), slice(u * LANES, (u + 1) * LANES)
        out_ref[0, 0, rows, lanes] = block[:, :LANES] * gains[at]
        out_ref[0, 1, rows, lanes] = block[:, LANES:] * gains[at]


def correlate(shares, spectrum, gain, patch, me_acq):
    parts = len(shares)
    _, share, cols = shares[0].shape
    vmem = pl.BlockSpec(memory_space=pltpu.VMEM)
    return pl.pallas_call(
        functools.partial(correlate_kernel, parts=parts),
        in_specs=[pl.BlockSpec(memory_space=pltpu.SMEM)] + [vmem] * (parts + 5),
        out_specs=vmem,
        out_shape=jax.ShapeDtypeStruct((1, 2, share * parts, cols), F32),
        scratch_shapes=[pltpu.VMEM((2, share * parts, cols), BF16)],
        compiler_params=pltpu.CompilerParams(vmem_limit_bytes=VMEM_BYTES),
        name="correlate",
    )(me_acq.reshape(1).astype(jnp.int32), *shares, spectrum, gain, *patch)


def trade(blocks, axis):
    devices = len(blocks)
    return [blocks[0]] + [
        lax.ppermute(blocks[k], axis, [(i, i ^ k) for i in range(devices)]) for k in range(1, devices)
    ]


def with_edges(array, axis):
    devices = lax.axis_size(axis)
    up = [(i, i + 1) for i in range(devices - 1)]
    down = [(i + 1, i) for i in range(devices - 1)]
    before = lax.ppermute(array[:, -LANES:], axis, up)
    after = lax.ppermute(array[:, :LANES], axis, down)
    return jnp.concatenate([before, array, after], axis=1)


def on_device(echo, filt, slope, centre, valid, reference, offsets):
    devices, parts = lax.axis_size("lines"), lax.axis_size("acq")
    me, me_acq = lax.axis_index("lines"), lax.axis_index("acq")
    lines = echo.shape[2] * devices
    matrices = azimuth_matrices(lines)
    patch = patch_matrices()
    inner, outer = compress(echo[0], filt[0], me, valid[0], devices)
    inner = trade(inner, "lines")
    outer = trade(outer, "lines")
    image, *shares = focus_inner(inner, slope, centre, matrices, me, me_acq, parts)
    shares = trade(shares, "acq")
    edged = with_edges(jnp.concatenate([slope, centre], axis=0), "lines")
    spectrum, gain = focus_outer(
        outer, image, edged[:1], edged[1:], matrices, patch, me, offsets[0]
    )
    source = me_acq ^ reference[0]
    mine = shares[0]
    for k in range(1, parts):
        mine = jnp.where(source == k, shares[k], mine)
    shares = trade([mine] * parts, "acq")
    return correlate(shares, spectrum, gain, patch, me_acq)


def solution(mesh):
    return jax.shard_map(
        on_device,
        mesh=mesh,
        in_specs=(
            P(("stack", "acq"), None, "lines", None),
            P(("stack", "acq"), None, None),
            P(("stack", "acq"), "lines"),
            P(("stack", "acq"), "lines"),
            P(("stack", "acq")),
            P("stack"),
            P(("stack", "acq"), None, None, "lines"),
        ),
        out_specs=P(("stack", "acq"), None, None, "lines"),
        check_vma=False,
    )
```

```python
import functools
import math

import jax
import jax.numpy as jnp
import ml_dtypes
import numpy as np
from jax import lax
from jax.experimental import pallas as pl
from jax.experimental.pallas import tpu as pltpu
from jax.sharding import PartitionSpec as P

PATCH = 64
LANES = 128
HALF = PATCH // 2
EPS = 1e-06
F32 = jnp.float32
BF16 = jnp.bfloat16
VMEM_BYTES = 32 * 1024 * 1024
RANGE_BYTES = 60 * 1024 * 1024

ROW_PARTS = 1
COLUMN_PARTS = 2

SIN_POLY = (3.141582022139052, -5.167142795074894, 2.541899011376644, -0.5546361478584824)
COS_POLY = (0.9999933027022169, -4.9339382503784215, 4.041285686469419, -1.2221312612719153)


def split_np(matrix):
    high = matrix.astype(ml_dtypes.bfloat16)
    low = (matrix - high.astype(np.float64)).astype(ml_dtypes.bfloat16)
    return high, low


def angle_np(rows, cols, period):
    return 2.0 * np.pi * ((np.asarray(rows)[:, None] * np.asarray(cols)[None, :]) % period) / period


def right_matrix(theta, sign, scale=1.0):
    cos, sin = np.cos(theta) * scale, sign * np.sin(theta) * scale
    return split_np(np.block([[cos, sin], [-sin, cos]]))


def left_matrix(theta, sign, scale=1.0):
    cos, sin = np.cos(theta) * scale, sign * np.sin(theta) * scale
    return split_np(np.block([[cos, -sin], [sin, cos]]))


def cost(microseconds):
    return pl.CostEstimate(
        flops=int(microseconds * 1e9), bytes_accessed=int(microseconds * 3.5e6), transcendentals=0
    )


def split(value):
    high = value.astype(BF16)
    low = (value - high.astype(F32)).astype(BF16)
    return high, low


def dot(lhs, rhs):
    return jnp.dot(lhs, rhs, preferred_element_type=F32)


def fft_list(re, im, sign):
    size = len(re)
    if size == 1:
        return re, im
    if size == 2:
        return [re[0] + re[1], re[0] - re[1]], [im[0] + im[1], im[0] - im[1]]
    even_re, even_im = fft_list(re[0::2], im[0::2], sign)
    odd_re, odd_im = fft_list(re[1::2], im[1::2], sign)
    half = size // 2
    out_re, out_im = [None] * size, [None] * size
    root = math.sqrt(0.5)
    for k in range(half):
        a, b = odd_re[k], odd_im[k]
        if k == 0:
            t_re, t_im = a, b
        elif 4 * k == size:
            t_re, t_im = (b, -a) if sign < 0 else (-b, a)
        elif 8 * k == size:
            t_re, t_im = ((a + b) * root, (b - a) * root) if sign < 0 else ((a - b) * root, (a + b) * root)
        elif 8 * k == 3 * size:
            t_re, t_im = ((b - a) * root, (a + b) * -root) if sign < 0 else ((a + b) * -root, (a - b) * root)
        else:
            cos = math.cos(2.0 * math.pi * k / size)
            sin = sign * math.sin(2.0 * math.pi * k / size)
            t_re, t_im = a * cos - b * sin, a * sin + b * cos
        if 4 * k == size:
            if sign < 0:
                out_re[k], out_re[k + half] = even_re[k] + b, even_re[k] - b
                out_im[k], out_im[k + half] = even_im[k] - a, even_im[k] + a
            else:
                out_re[k], out_re[k + half] = even_re[k] - b, even_re[k] + b
                out_im[k], out_im[k + half] = even_im[k] + a, even_im[k] - a
            continue
        out_re[k], out_re[k + half] = even_re[k] + t_re, even_re[k] - t_re
        out_im[k], out_im[k + half] = even_im[k] + t_im, even_im[k] - t_im
    return out_re, out_im


def three_pass(lhs, high, low):
    lhs_high, lhs_low = lhs
    return dot(lhs_high, high) + dot(lhs_low, high) + dot(lhs_high, low)


def spread_filter(filt_ref, out):
    count = out.shape[1]
    for part in range(2):
        rows = [filt_ref[part : part + 1, a * LANES : (a + 1) * LANES] for a in range(count)]
        rows.append(jnp.zeros((LANES - count, LANES), F32))
        turned = jnp.concatenate(rows, axis=0).T
        out[part] = jnp.concatenate(
            [turned[e * count : (e + 1) * count, :count] for e in range(LANES // count)], axis=1
        )


def edge_rows(slope_ref, centre_ref):
    lane = lax.broadcasted_iota(jnp.int32, (1, LANES), 1)
    rows = []
    for ref in (slope_ref, centre_ref):
        value = jnp.where(lane < 96, pltpu.roll(ref[:, :LANES], 64, 1), ref[:, -LANES:])
        for _ in range(3):
            part = value.astype(BF16).astype(F32)
            rows.append(part)
            value = value - part
    return jnp.concatenate(rows + [jnp.zeros((16 - len(rows), LANES), F32)], axis=0)


def range_kernel(valid, x_ref, filter_ref, slope_ref, centre_ref, tw_ref, mat_ref, *rest, devices, first, chunks, held):
    rest = rest[held:]
    outs, (in_scr, out_scr, filt_ref) = rest[:-3], rest[-3:]
    inner_refs = [outs[k * len(chunks) : (k + 1) * len(chunks)] for k in range(devices)]
    outer_refs = outs[devices * len(chunks) :]
    rows, length = x_ref.shape[1], x_ref.shape[2]
    count = length // LANES
    half = count // devices // 2
    me = lax.axis_index("lines")
    sub = 8

    @pl.when(pl.program_id(0) == 0)
    def _():
        spread_filter(filter_ref, filt_ref)

    base = me * first[1] + first[0] + pl.program_id(0) * rows
    lane = lax.broadcasted_iota(jnp.int32, (sub, LANES), 1)
    for block in range(rows // sub):
        span = slice(block * sub, (block + 1) * sub)
        keep = base + block * sub + lax.broadcasted_iota(jnp.int32, (sub, LANES), 0) < valid[0]
        re, im = [], []
        for a in range(count):
            at = slice(a * LANES, (a + 1) * LANES)
            re.append(jnp.where(keep, x_ref[0, span, at].astype(F32), 0.0))
            im.append(jnp.where(keep, x_ref[1, span, at].astype(F32), 0.0))
        re, im = fft_list(re, im, -1)
        mixed = []
        for c in range(count):
            cos, sin = tw_ref[0, c : c + 1, :], tw_ref[1, c : c + 1, :]
            mixed.append(jnp.concatenate([re[c] * cos - im[c] * sin, re[c] * sin + im[c] * cos], axis=1))
        spectrum = three_pass(split(jnp.concatenate(mixed, 0)), mat_ref[0], mat_ref[1])
        mixed = []
        for c in range(count):
            at = slice(c * sub, (c + 1) * sub)
            a, b = spectrum[at, :LANES], spectrum[at, LANES:]
            cos, sin = filt_ref[0, c : c + 1, :], filt_ref[1, c : c + 1, :]
            mixed.append(jnp.concatenate([a * cos - b * sin, a * sin + b * cos], axis=1))
        pulse = three_pass(split(jnp.concatenate(mixed, 0)), mat_ref[2], mat_ref[3])
        re, im = [], []
        for c in range(count):
            at = slice(c * sub, (c + 1) * sub)
            a, b = pulse[at, :LANES], pulse[at, LANES:]
            cos, sin = tw_ref[2, c : c + 1, :], tw_ref[3, c : c + 1, :]
            re.append(a * cos - b * sin)
            im.append(a * sin + b * cos)
        parts = fft_list(re, im, 1)
        zero = jnp.zeros((sub, LANES), F32)
        for part in range(2):
            y = parts[part]
            group = [jnp.where(lane < 96, y[a - 1] if a else zero, y[a] if a < count else zero) for a in range(count + 1)]
            group.append(zero)
            for u in range(count // 2):
                in_scr[u, part, span, :] = jnp.where(
                    lane < 64, y[2 * u], pltpu.roll(y[2 * u + 1], 64, 1)
                )
            for u in range(count // 2 + 1):
                out_scr[u, part, span, :] = jnp.where(
                    lane < 64, pltpu.roll(group[2 * u], 64, 1), group[2 * u + 1]
                )
    for k in range(devices):
        start = (me ^ k) * half
        at = 0
        for refs, tiles in zip(inner_refs[k], chunks):
            for t in range(tiles):
                refs[:, :, t * LANES : (t + 1) * LANES] = in_scr[start + at + t].astype(BF16)
            at += tiles
        for t in range(half + 1):
            outer_refs[k][:, :, t * LANES : (t + 1) * LANES] = out_scr[start + t].astype(BF16)
    if first[0] == 0:

        @pl.when(pl.program_id(0) == 0)
        def _():
            edge = edge_rows(slope_ref, centre_ref)
            wide = lax.broadcasted_iota(jnp.int32, (16, LANES), 1)
            for k in range(devices):
                at = slice(half * LANES, (half + 1) * LANES)
                known = outer_refs[k][0, :16, at].astype(F32)
                outer_refs[k][0, :16, at] = jnp.where(wide < 64, known, edge).astype(BF16)


def compress(echo, filt, slope, centre, valid, devices, part, parts, chunks, outer):
    _, rows, length = echo.shape
    count = length // LANES
    half = count // devices // 2
    mine = rows // parts
    step = min(64, mine)
    steps = mine // step
    natural = np.arange(LANES)
    turned = (natural + HALF) % LANES
    q = LANES // count
    freq = q * (natural % count) + natural // count
    twf = -angle_np(np.arange(count), natural, length)
    twi = angle_np(np.arange(count), turned, length)
    twiddles = np.stack([np.cos(twf), np.sin(twf), np.cos(twi), np.sin(twi)])
    mats = right_matrix(angle_np(natural, freq, LANES), -1) + right_matrix(
        angle_np(freq, turned, LANES), 1, 1.0 / length
    )
    inner_widths = [c * LANES for c in chunks] * devices
    width = (half + 1) * LANES
    outs = pl.pallas_call(
        functools.partial(
            range_kernel, devices=devices, first=(part * mine, rows), chunks=chunks, held=len(outer)
        ),
        grid=(steps,),
        in_specs=[
            pl.BlockSpec(memory_space=pltpu.SMEM),
            pl.BlockSpec((2, step, length), lambda i: (0, part * steps + i, 0)),
            pl.BlockSpec((2, length), lambda i: (0, 0)),
            pl.BlockSpec(slope.shape, lambda i: (0, 0)),
            pl.BlockSpec(slope.shape, lambda i: (0, 0)),
            pl.BlockSpec((4, count, LANES), lambda i: (0, 0, 0)),
            pl.BlockSpec((4, 2 * LANES, 2 * LANES), lambda i: (0, 0, 0)),
        ]
        + [pl.BlockSpec(memory_space=pl.ANY)] * len(outer),
        out_specs=[pl.BlockSpec((2, step, w), lambda i: (0, i, 0)) for w in inner_widths]
        + [pl.BlockSpec((2, step, width), lambda i: (0, part * steps + i, 0))] * devices,
        scratch_shapes=[
            pltpu.VMEM((count // 2, 2, step, LANES), F32),
            pltpu.VMEM((count // 2 + 1, 2, step, LANES), F32),
            pltpu.VMEM((2, count, LANES), F32),
        ],
        out_shape=[jax.ShapeDtypeStruct((2, mine, w), BF16) for w in inner_widths]
        + [jax.ShapeDtypeStruct((2, rows, width), BF16)] * devices,
        input_output_aliases={7 + k: len(inner_widths) + k for k in range(len(outer))},
        compiler_params=pltpu.CompilerParams(vmem_limit_bytes=RANGE_BYTES),
        cost_estimate=cost(9.0 / parts),
        name="range_compress",
    )(valid, echo, filt, slope, centre, jnp.asarray(twiddles, F32), jnp.asarray(np.stack(mats)), *outer)
    inner = [outs[k * len(chunks) : (k + 1) * len(chunks)] for k in range(devices)]
    return inner, outs[len(inner_widths) :]


def turn(turns):
    x = turns - jnp.round(turns)
    z = x * x
    a, b = [v * math.sqrt(2.0) for v in SIN_POLY], [v * math.sqrt(2.0) for v in COS_POLY]
    sin = x * (a[0] + z * (a[1] + z * (a[2] + z * a[3])))
    cos = b[0] + z * (b[1] + z * (b[2] + z * b[3]))
    return 1.0 - sin * sin, sin * cos


def focus_tile(scr, col, width, slope, centre, af_ref, ai_ref):
    lines = scr.shape[1]
    radix = lines // LANES
    at = slice(col, col + width)
    re = [scr[0, s * LANES : (s + 1) * LANES, at].astype(F32) for s in range(radix)]
    im = [scr[1, s * LANES : (s + 1) * LANES, at].astype(F32) for s in range(radix)]
    re, im = fft_list(re, im, -1)
    k = radix * lax.broadcasted_iota(jnp.int32, (LANES, width), 0)
    u = jnp.where(k >= lines // 2, k - lines, k).astype(F32) * (1.0 / lines)
    back_re, back_im = [], []
    rate = slope * (lines / 8.0)
    for c in range(radix):
        high, low = split(jnp.concatenate([re[c], im[c]], axis=0))
        freq = dot(af_ref[0, c], high) + dot(af_ref[0, c], low) + dot(af_ref[1, c], high)
        w = u - (centre - c / lines)
        cos, sin = turn(rate * w * w)
        a, b = freq[:LANES], freq[LANES:]
        high, low = split(jnp.concatenate([a * cos - b * sin, a * sin + b * cos], axis=0))
        back = dot(ai_ref[0, c], high) + dot(ai_ref[0, c], low) + dot(ai_ref[1, c], high)
        back_re.append(back[:LANES])
        back_im.append(back[LANES:])
    return fft_list(back_re, back_im, 1)


def azimuth_matrices(lines):
    radix = lines // LANES
    t = np.arange(LANES)
    forward, inverse = [], []
    for c in range(radix):
        k = c + radix * t
        forward.append(np.stack(left_matrix(angle_np(k, t, lines), -1)))
        inverse.append(np.stack(left_matrix(angle_np(t, k, lines), 1, 1.0 / lines)))
    return jnp.asarray(np.stack(forward, axis=1)), jnp.asarray(np.stack(inverse, axis=1))


def gather_lines(blocks, scr):
    me = lax.axis_index("lines")
    devices = len(blocks)
    rows = scr.shape[1] // devices
    for k, parts in enumerate(blocks):
        share = rows // len(parts)
        for h, part in enumerate(parts):
            start = pl.multiple_of((me ^ k) * rows + h * share, share)
            scr[:, pl.ds(start, share), :] = part[...]


def nested(refs, devices):
    per = len(refs) // devices
    return [refs[k * per : (k + 1) * per] for k in range(devices)]


def inner_kernel(*rest, devices, row_parts, parts):
    blocks, rest = nested(rest[: devices * row_parts], devices), rest[devices * row_parts :]
    slope_ref, centre_ref, af_ref, ai_ref, out_ref = rest[:5]
    p_refs, (scr, p_scr) = rest[5 : 5 + parts], rest[5 + parts :]
    gather_lines(blocks, scr)
    width = out_ref.shape[2]
    lane = lax.broadcasted_iota(jnp.int32, (1, LANES), 1)

    def packed(ref):
        tiles = []
        for t in range(width // LANES):
            a = pltpu.roll(ref[:, 2 * t * LANES : (2 * t + 1) * LANES], 96, 1)
            b = pltpu.roll(ref[:, (2 * t + 1) * LANES : (2 * t + 2) * LANES], 32, 1)
            tiles.append(jnp.where(lane < 64, a, b))
        return jnp.concatenate(tiles, axis=1)

    re, im = focus_tile(scr, 0, width, packed(slope_ref), packed(centre_ref), af_ref, ai_ref)
    for part, value in enumerate((re, im)):
        for s in range(len(value)):
            image = value[s].astype(BF16)
            out_ref[part, s * LANES : (s + 1) * LANES, :] = image
            p_scr[part, s * PATCH : (s + 1) * PATCH, :] = image[HALF : HALF + PATCH]
    share = p_scr.shape[1] // parts
    me = lax.axis_index("acq") if parts > 1 else 0
    for k in range(parts):
        start = pl.multiple_of((me ^ k) * share, share)
        p_refs[k][...] = p_scr[:, pl.ds(start, share), :]


def focus_inner(blocks, slope, centre, matrices, first, parts):
    devices, row_parts = len(blocks), len(blocks[0])
    _, rows, cols = blocks[0][0].shape
    lines = rows * devices * row_parts
    tile = 2 * LANES if cols % (2 * LANES) == 0 else LANES
    skip = first * LANES // (2 * tile)
    prows = lines // 2
    shape = (2, lines // LANES, 2 * LANES, 2 * LANES)
    return pl.pallas_call(
        functools.partial(inner_kernel, devices=devices, row_parts=row_parts, parts=parts),
        grid=(cols // tile,),
        in_specs=[pl.BlockSpec((2, rows, tile), lambda i: (0, 0, i))] * (devices * row_parts)
        + [pl.BlockSpec((1, 2 * tile), lambda i: (0, skip + i))] * 2
        + [pl.BlockSpec(shape, lambda i: (0, 0, 0, 0))] * 2,
        out_specs=[pl.BlockSpec((2, lines, tile), lambda i: (0, 0, i))]
        + [pl.BlockSpec((2, prows // parts, tile), lambda i: (0, 0, i))] * parts,
        scratch_shapes=[pltpu.VMEM((2, lines, tile), BF16), pltpu.VMEM((2, prows, tile), BF16)],
        out_shape=[jax.ShapeDtypeStruct((2, lines, cols), BF16)]
        + [jax.ShapeDtypeStruct((2, prows // parts, cols), BF16)] * parts,
        compiler_params=pltpu.CompilerParams(vmem_limit_bytes=VMEM_BYTES),
        cost_estimate=cost(0.8 * cols / LANES),
        name="focus_inner",
    )(*[part for parts_of in blocks for part in parts_of], slope, centre, *matrices)


def outer_kernel(*rest, devices):
    blocks, rest = rest[:devices], rest[devices:]
    slope_ref, centre_ref, af_ref, ai_ref, out_ref, scr = rest
    gather_lines([[b] for b in blocks], scr)
    width = scr.shape[2]
    lane = lax.broadcasted_iota(jnp.int32, (1, LANES), 1)
    pairs = width // LANES - 1

    me = lax.axis_index("lines")

    def extended(ref, row):
        before = after = jnp.zeros((1, LANES), F32)
        for k in range(1, devices):
            told = blocks[k][0, :16, pairs * LANES :].astype(F32)
            told = told[row : row + 1] + told[row + 1 : row + 2] + told[row + 2 : row + 3]
            before = jnp.where((me ^ k) == me - 1, told, before)
            after = jnp.where((me ^ k) == me + 1, pltpu.roll(told, 64, 1), after)
        return [before] + [ref[:, t * LANES : (t + 1) * LANES] for t in range(ref.shape[1] // LANES)] + [after]

    def group(values, a):
        return jnp.where(lane < 96, pltpu.roll(values[a], 96, 1), pltpu.roll(values[a + 1], 96, 1))

    def packed(values, u):
        left = pltpu.roll(group(values, 2 * u), 64, 1)
        if u == pairs:
            return jnp.where(lane < 64, left, 0.0)
        return jnp.where(lane < 64, left, group(values, 2 * u + 1))

    slopes, centres = extended(slope_ref, 0), extended(centre_ref, 3)
    u = 0
    while u <= pairs:
        tiles = min(2, pairs + 1 - u)
        slope = jnp.concatenate([packed(slopes, u + t) for t in range(tiles)], axis=1)
        centre = jnp.concatenate([packed(centres, u + t) for t in range(tiles)], axis=1)
        at = slice(u * LANES, (u + tiles) * LANES)
        for part, value in enumerate(focus_tile(scr, u * LANES, tiles * LANES, slope, centre, af_ref, ai_ref)):
            for s in range(len(value)):
                out_ref[part, s * LANES : (s + 1) * LANES, at] = value[s].astype(BF16)
        u += tiles


def focus_outer(blocks, slope, centre, matrices):
    devices = len(blocks)
    _, rows, cols = blocks[0].shape
    lines = rows * devices
    vmem = pl.BlockSpec(memory_space=pltpu.VMEM)
    return pl.pallas_call(
        functools.partial(outer_kernel, devices=devices),
        in_specs=[vmem] * (devices + 4),
        out_specs=vmem,
        out_shape=jax.ShapeDtypeStruct((2, lines, cols), BF16),
        scratch_shapes=[pltpu.VMEM((2, lines, cols), BF16)],
        compiler_params=pltpu.CompilerParams(vmem_limit_bytes=VMEM_BYTES),
        cost_estimate=cost(4.0),
        name="focus_outer",
    )(*blocks, slope, centre, *matrices)


def patch_matrices():
    n = np.arange(PATCH)
    theta = angle_np(n, n, PATCH)

    def lanes(sign):
        cos = np.kron(np.eye(2), np.cos(theta))
        sin = sign * np.kron(np.eye(2), np.sin(theta))
        return np.stack(split_np(np.block([[cos, sin], [-sin, cos]])))

    high, low = split_np(np.concatenate([np.cos(theta), np.sin(theta)], axis=0))
    column = np.concatenate([high, high, low], axis=1)
    return jnp.asarray(lanes(-1)), jnp.asarray(lanes(1)), jnp.asarray(column)


def columns(value, column_ref, sign):
    high, low = split(value)
    both = dot(column_ref[...], jnp.concatenate([high, low, high], axis=0))
    c_re, c_im = both[:PATCH, :LANES], both[:PATCH, LANES:]
    s_re, s_im = both[PATCH:, :LANES], both[PATCH:, LANES:]
    if sign < 0:
        return c_re + s_im, c_im - s_re
    return c_re - s_im, c_im + s_re


def power(re, im):
    lane = lax.broadcasted_iota(jnp.int32, (1, LANES), 1)
    total = jnp.sum(re * re + im * im, axis=0, keepdims=True)
    left = jnp.sum(jnp.where(lane < PATCH, total, 0.0), axis=1, keepdims=True)
    right = jnp.sum(jnp.where(lane < PATCH, 0.0, total), axis=1, keepdims=True)
    return jnp.where(lane < PATCH, left, right) * (1.0 / (PATCH * PATCH))


def window_kernel(offsets, *rest, chunks):
    inner_refs, rest = rest[: len(chunks)], rest[len(chunks) :]
    outer_ref, lane_ref, column_ref = rest[:3]
    spec_ref, image, windows = rest[3:]
    lines, pairs = outer_ref.shape[1], outer_ref.shape[2] // LANES - 1
    lane = lax.broadcasted_iota(jnp.int32, (1, LANES), 1)
    edge = jnp.zeros((HALF, image.shape[2]), F32)
    for part in range(2):
        image[part, :HALF, :] = edge
        image[part, HALF + lines : 2 * HALF + lines, :] = edge
    where = [(c, t) for c, tiles in enumerate(chunks) for t in range(tiles)]
    for u in range(pairs + 1):
        for part in range(2):
            fresh = outer_ref[part, :, u * LANES : (u + 1) * LANES].astype(F32)
            at = slice(HALF, HALF + lines)
            if u == pairs:
                image[part, at, 2 * u * LANES : (2 * u + 1) * LANES] = fresh
                continue
            c, t = where[u]
            known = inner_refs[c][part, :, t * LANES : (t + 1) * LANES].astype(F32)
            image[part, at, 2 * u * LANES : (2 * u + 1) * LANES] = jnp.where(
                lane < 64, fresh, pltpu.roll(known, 64, 1)
            )
            image[part, at, (2 * u + 1) * LANES : (2 * u + 2) * LANES] = jnp.where(
                lane < 64, pltpu.roll(fresh, 64, 1), known
            )
    row_blocks = lines // (2 * PATCH)
    wide = lax.broadcasted_iota(jnp.int32, (PATCH + 8, LANES), 1)

    def block(i, carry):
        gains = []
        for u in range(pairs):
            found = [[], []]
            for side in range(2):
                j = 2 * u + side
                start = 2 * PATCH * i + PATCH + offsets[0, i, j]
                shift = PATCH + offsets[1, i, j]
                back = jnp.bitwise_and(2 * LANES - shift + side * PATCH, LANES - 1)
                base = pl.multiple_of(lax.shift_left(lax.shift_right_logical(start, 3), 3), 8)
                up = PATCH + 8 - jnp.bitwise_and(start, 7)
                for part in range(2):
                    left = image[part, pl.ds(base, PATCH + 8), j * LANES : (j + 1) * LANES]
                    right = image[part, pl.ds(base, PATCH + 8), (j + 1) * LANES : (j + 2) * LANES]
                    turned = pltpu.roll(jnp.where(wide >= shift, left, right), back, 1)
                    found[part].append(pltpu.roll(turned, up, 0)[:PATCH])
            re = jnp.where(lane < PATCH, found[0][0], found[0][1])
            im = jnp.where(lane < PATCH, found[1][0], found[1][1])
            gains.append(lax.rsqrt(power(re, im) + EPS) * (1.0 / PATCH**3))
            windows[u * PATCH : (u + 1) * PATCH, :] = jnp.concatenate([re, im], axis=1).astype(BF16)
        mixed = dot(windows[...], lane_ref[0]) + dot(windows[...], lane_ref[1])
        for u in range(pairs):
            re, im = columns(mixed[u * PATCH : (u + 1) * PATCH], column_ref, -1)
            spec_ref[0, i * pairs + u] = re * gains[u]
            spec_ref[1, i * pairs + u] = im * gains[u]
        return carry

    lax.fori_loop(0, row_blocks, block, 0)


def window_spectra(inner, outer, patch, offsets, chunks):
    lines, pairs = outer.shape[1], outer.shape[2] // LANES - 1
    vmem = pl.BlockSpec(memory_space=pltpu.VMEM)
    return pl.pallas_call(
        functools.partial(window_kernel, chunks=chunks),
        in_specs=[pl.BlockSpec(memory_space=pltpu.SMEM)] + [vmem] * (len(chunks) + 3),
        out_specs=vmem,
        out_shape=jax.ShapeDtypeStruct((2, lines // (2 * PATCH) * pairs, PATCH, LANES), F32),
        scratch_shapes=[
            pltpu.VMEM((2, lines + 2 * HALF + 8, (2 * pairs + 1) * LANES), F32),
            pltpu.VMEM((pairs * PATCH, 2 * LANES), BF16),
        ],
        compiler_params=pltpu.CompilerParams(vmem_limit_bytes=VMEM_BYTES),
        cost_estimate=cost(4.0),
        name="window_spectra",
    )(offsets, *inner, outer, patch[0], patch[2])


def primary_kernel(reference, *rest, parts):
    shares, (lane_ref, column_ref, out_ref, scr) = rest[:-4], rest[-4:]
    source = lax.axis_index("acq") ^ reference[0] if parts > 1 else 0
    for k in range(parts):

        @pl.when(source == k)
        def _(k=k):
            col = 0
            for ref in shares[k::parts]:
                scr[:, :, col : col + ref.shape[2]] = ref[...]
                col += ref.shape[2]

    rows, cols = scr.shape[1], scr.shape[2]
    for u in range(cols // LANES):
        lanes = slice(u * LANES, (u + 1) * LANES)
        both = jnp.concatenate([scr[0, :, lanes], scr[1, :, lanes]], axis=1)
        mixed = dot(both, lane_ref[0]) + dot(both, lane_ref[1])
        for i in range(rows // PATCH):
            at = slice(i * PATCH, (i + 1) * PATCH)
            value = both[at].astype(F32)
            gain = lax.rsqrt(power(value[:, :LANES], value[:, LANES:]) + EPS)
            re, im = columns(mixed[at], column_ref, -1)
            out_ref[0, at, lanes] = (re * gain).astype(BF16)
            out_ref[1, at, lanes] = (im * gain).astype(BF16)


def primary_spectra(reference, shares, patch):
    vmem = pl.BlockSpec(memory_space=pltpu.VMEM)
    flat = [share for chunk in shares for share in chunk]
    shape = flat[0].shape[:2] + (sum(chunk[0].shape[2] for chunk in shares),)
    return pl.pallas_call(
        functools.partial(primary_kernel, parts=len(shares[0])),
        in_specs=[pl.BlockSpec(memory_space=pltpu.SMEM)] + [vmem] * (len(flat) + 2),
        out_specs=vmem,
        out_shape=jax.ShapeDtypeStruct(shape, BF16),
        scratch_shapes=[pltpu.VMEM(shape, BF16)],
        compiler_params=pltpu.CompilerParams(vmem_limit_bytes=VMEM_BYTES),
        cost_estimate=cost(1.0),
        name="primary_spectra",
    )(reference, *flat, patch[0], patch[2])


def correlate_kernel(*rest, parts):
    shares, (spec_ref, inverse_ref, column_ref, out_ref) = rest[:parts], rest[parts:]
    _, rows, cols = shares[0].shape
    pairs = cols // LANES
    per = rows // PATCH
    me = lax.axis_index("acq") if parts > 1 else 0
    for k in range(parts):
        for r in range(per):
            i = (me ^ k) * per + r
            middle = []
            for u in range(pairs):
                at, lanes = slice(r * PATCH, (r + 1) * PATCH), slice(u * LANES, (u + 1) * LANES)
                p_re, p_im = shares[k][0, at, lanes].astype(F32), shares[k][1, at, lanes].astype(F32)
                s_re, s_im = spec_ref[0, i * pairs + u], spec_ref[1, i * pairs + u]
                cross = jnp.concatenate([p_re * s_re + p_im * s_im, p_im * s_re - p_re * s_im], axis=1)
                middle.append(jnp.concatenate(columns(cross, column_ref, 1), axis=1))
            surface = three_pass(split(jnp.concatenate(middle, axis=0)), inverse_ref[0], inverse_ref[1])
            line = pl.ds(pl.multiple_of(i * PATCH, PATCH), PATCH)
            for u in range(pairs):
                lanes = slice(u * LANES, (u + 1) * LANES)
                block = surface[u * PATCH : (u + 1) * PATCH]
                out_ref[0, 0, line, lanes] = block[:, :LANES]
                out_ref[0, 1, line, lanes] = block[:, LANES:]


def correlate(shares, spectrum, patch):
    parts = len(shares)
    _, rows, cols = shares[0].shape
    vmem = pl.BlockSpec(memory_space=pltpu.VMEM)
    return pl.pallas_call(
        functools.partial(correlate_kernel, parts=parts),
        in_specs=[vmem] * (parts + 3),
        out_specs=vmem,
        out_shape=jax.ShapeDtypeStruct((1, 2, rows * parts, cols), F32),
        compiler_params=pltpu.CompilerParams(vmem_limit_bytes=VMEM_BYTES),
        cost_estimate=cost(2.0),
        name="correlate",
    )(*shares, spectrum, patch[1], patch[2])


def far_first(devices):
    return list(range(2, devices)) + list(range(min(2, devices)))[::-1]


def trade(block, k, axis):
    if k == 0:
        return block
    return lax.ppermute(block, axis, [(i, i ^ k) for i in range(lax.axis_size(axis))])


def on_device(echo, filt, slope, centre, valid, reference, offsets):
    devices, parts = lax.axis_size("lines"), lax.axis_size("acq")
    rows, length = echo.shape[2], echo.shape[3]
    lines = rows * devices
    tiles = length // devices // (2 * LANES)
    chunks = (tiles // COLUMN_PARTS,) * COLUMN_PARTS if tiles % COLUMN_PARTS == 0 else (tiles,)
    row_parts = ROW_PARTS if rows % (32 * ROW_PARTS) == 0 else 1
    spread = lines // (2 * PATCH) % parts == 0
    matrices = azimuth_matrices(lines)
    patch = patch_matrices()
    inner = [[[] for _ in range(devices)] for _ in chunks]
    outer = []
    for h in range(row_parts):
        mine, outer = compress(echo[0], filt[0], slope, centre, valid, devices, h, row_parts, chunks, outer)
        for c in range(len(chunks)):
            for k in far_first(devices):
                inner[c][k].append(trade(mine[k][c], k, "lines"))
    outer = {k: trade(outer[k], k, "lines") for k in far_first(devices)}
    outer = [outer[k] for k in range(devices)]
    if len(inner) > 1:
        inner[-1], outer[1] = lax.optimization_barrier((inner[-1], outer[1]))
    images, primaries = [], []
    for c in range(len(chunks)):
        image, *shares = focus_inner(
            inner[c], slope, centre, matrices, 2 * sum(chunks[:c]), parts if spread else 1
        )
        images.append(image)
        if spread:
            shares = {k: trade(shares[k], k, "acq") for k in far_first(parts)}
            shares = [shares[k] for k in range(parts)]
        else:
            mine = lax.axis_index("acq") == reference[0]
            shares = [lax.psum(jnp.where(mine, shares[0], 0).astype(BF16), "acq")]
        primaries.append(shares)
    outer = focus_outer(outer, slope, centre, matrices)
    spectrum = window_spectra(images, outer, patch, offsets[0], chunks)
    shares = [primary_spectra(reference, primaries, patch)]
    for k in range(1, parts if spread else 1):
        low = k & -k
        shares.append(trade(shares[k - low], low, "acq"))
    return correlate(shares, spectrum, patch)


def solution(mesh):
    return jax.shard_map(
        on_device,
        mesh=mesh,
        in_specs=(
            P(("stack", "acq"), None, "lines", None),
            P(("stack", "acq"), None, None),
            P(("stack", "acq"), "lines"),
            P(("stack", "acq"), "lines"),
            P(("stack", "acq")),
            P("stack"),
            P(("stack", "acq"), None, None, "lines"),
        ),
        out_specs=P(("stack", "acq"), None, None, "lines"),
        check_vma=False,
    )
```

```python
import functools
import math

import jax
import jax.numpy as jnp
import ml_dtypes
import numpy as np
from jax import lax
from jax.experimental import pallas as pl
from jax.experimental.pallas import tpu as pltpu
from jax.sharding import PartitionSpec as P

PATCH = 64
LANES = 128
HALF = PATCH // 2
EPS = 1e-06
F32 = jnp.float32
BF16 = jnp.bfloat16
VMEM_BYTES = 32 * 1024 * 1024
RANGE_BYTES = 60 * 1024 * 1024

ROW_PARTS = 1
COLUMN_PARTS = 2

SIN_POLY = (3.141582022139052, -5.167142795074894, 2.541899011376644, -0.5546361478584824)
COS_POLY = (0.9999933027022169, -4.9339382503784215, 4.041285686469419, -1.2221312612719153)


def split_np(matrix):
    high = matrix.astype(ml_dtypes.bfloat16)
    low = (matrix - high.astype(np.float64)).astype(ml_dtypes.bfloat16)
    return high, low


def angle_np(rows, cols, period):
    return 2.0 * np.pi * ((np.asarray(rows)[:, None] * np.asarray(cols)[None, :]) % period) / period


def right_matrix(theta, sign, scale=1.0):
    cos, sin = np.cos(theta) * scale, sign * np.sin(theta) * scale
    return split_np(np.block([[cos, sin], [-sin, cos]]))


def left_matrix(theta, sign, scale=1.0):
    cos, sin = np.cos(theta) * scale, sign * np.sin(theta) * scale
    return split_np(np.block([[cos, -sin], [sin, cos]]))


def cost(microseconds):
    return pl.CostEstimate(
        flops=int(microseconds * 1e9), bytes_accessed=int(microseconds * 3.5e6), transcendentals=0
    )


def split(value):
    high = value.astype(BF16)
    low = (value - high.astype(F32)).astype(BF16)
    return high, low


def dot(lhs, rhs):
    return jnp.dot(lhs, rhs, preferred_element_type=F32)


def fft_list(re, im, sign):
    size = len(re)
    if size == 1:
        return re, im
    if size == 2:
        return [re[0] + re[1], re[0] - re[1]], [im[0] + im[1], im[0] - im[1]]
    even_re, even_im = fft_list(re[0::2], im[0::2], sign)
    odd_re, odd_im = fft_list(re[1::2], im[1::2], sign)
    half = size // 2
    out_re, out_im = [None] * size, [None] * size
    root = math.sqrt(0.5)
    for k in range(half):
        a, b = odd_re[k], odd_im[k]
        if k == 0:
            t_re, t_im = a, b
        elif 4 * k == size:
            t_re, t_im = (b, -a) if sign < 0 else (-b, a)
        elif 8 * k == size:
            t_re, t_im = ((a + b) * root, (b - a) * root) if sign < 0 else ((a - b) * root, (a + b) * root)
        elif 8 * k == 3 * size:
            t_re, t_im = ((b - a) * root, (a + b) * -root) if sign < 0 else ((a + b) * -root, (a - b) * root)
        else:
            cos = math.cos(2.0 * math.pi * k / size)
            sin = sign * math.sin(2.0 * math.pi * k / size)
            t_re, t_im = a * cos - b * sin, a * sin + b * cos
        if 4 * k == size:
            if sign < 0:
                out_re[k], out_re[k + half] = even_re[k] + b, even_re[k] - b
                out_im[k], out_im[k + half] = even_im[k] - a, even_im[k] + a
            else:
                out_re[k], out_re[k + half] = even_re[k] - b, even_re[k] + b
                out_im[k], out_im[k + half] = even_im[k] + a, even_im[k] - a
            continue
        out_re[k], out_re[k + half] = even_re[k] + t_re, even_re[k] - t_re
        out_im[k], out_im[k + half] = even_im[k] + t_im, even_im[k] - t_im
    return out_re, out_im


def three_pass(lhs, high, low):
    lhs_high, lhs_low = lhs
    return dot(lhs_high, high) + dot(lhs_low, high) + dot(lhs_high, low)


def spread_filter(filt_ref, out):
    count = out.shape[1]
    for part in range(2):
        rows = [filt_ref[part : part + 1, a * LANES : (a + 1) * LANES] for a in range(count)]
        rows.append(jnp.zeros((LANES - count, LANES), F32))
        turned = jnp.concatenate(rows, axis=0).T
        out[part] = jnp.concatenate(
            [turned[e * count : (e + 1) * count, :count] for e in range(LANES // count)], axis=1
        )


def edge_rows(slope_ref, centre_ref):
    lane = lax.broadcasted_iota(jnp.int32, (1, LANES), 1)
    rows = []
    for ref in (slope_ref, centre_ref):
        value = jnp.where(lane < 96, pltpu.roll(ref[:, :LANES], 64, 1), ref[:, -LANES:])
        for _ in range(3):
            part = value.astype(BF16).astype(F32)
            rows.append(part)
            value = value - part
    return jnp.concatenate(rows + [jnp.zeros((16 - len(rows), LANES), F32)], axis=0)


def range_kernel(valid, x_ref, filter_ref, slope_ref, centre_ref, tw_ref, mat_ref, *rest, devices, first, chunks, held):
    rest = rest[held:]
    outs, (in_scr, out_scr, filt_ref) = rest[:-3], rest[-3:]
    inner_refs = [outs[k * len(chunks) : (k + 1) * len(chunks)] for k in range(devices)]
    outer_refs = outs[devices * len(chunks) :]
    rows, length = x_ref.shape[1], x_ref.shape[2]
    count = length // LANES
    half = count // devices // 2
    me = lax.axis_index("lines")
    sub = 8

    @pl.when(pl.program_id(0) == 0)
    def _():
        spread_filter(filter_ref, filt_ref)

    base = me * first[1] + first[0] + pl.program_id(0) * rows
    lane = lax.broadcasted_iota(jnp.int32, (sub, LANES), 1)
    for block in range(rows // sub):
        span = slice(block * sub, (block + 1) * sub)
        odd = block * sub % 16
        whole = slice(block * sub - odd, block * sub - odd + 16)
        keep = base + block * sub + lax.broadcasted_iota(jnp.int32, (sub, LANES), 0) < valid[0]
        re, im = [], []
        for a in range(count):
            at = slice(a * LANES, (a + 1) * LANES)
            re.append(jnp.where(keep, x_ref[0, whole, at].astype(F32)[odd : odd + sub], 0.0))
            im.append(jnp.where(keep, x_ref[1, whole, at].astype(F32)[odd : odd + sub], 0.0))
        re, im = fft_list(re, im, -1)
        mixed = []
        for c in range(count):
            cos, sin = tw_ref[0, c : c + 1, :], tw_ref[1, c : c + 1, :]
            mixed.append(jnp.concatenate([re[c] * cos - im[c] * sin, re[c] * sin + im[c] * cos], axis=1))
        spectrum = three_pass(split(jnp.concatenate(mixed, 0)), mat_ref[0], mat_ref[1])
        mixed = []
        for c in range(count):
            at = slice(c * sub, (c + 1) * sub)
            a, b = spectrum[at, :LANES], spectrum[at, LANES:]
            cos, sin = filt_ref[0, c : c + 1, :], filt_ref[1, c : c + 1, :]
            mixed.append(jnp.concatenate([a * cos - b * sin, a * sin + b * cos], axis=1))
        pulse = three_pass(split(jnp.concatenate(mixed, 0)), mat_ref[2], mat_ref[3])
        re, im = [], []
        for c in range(count):
            at = slice(c * sub, (c + 1) * sub)
            a, b = pulse[at, :LANES], pulse[at, LANES:]
            cos, sin = tw_ref[2, c : c + 1, :], tw_ref[3, c : c + 1, :]
            re.append(a * cos - b * sin)
            im.append(a * sin + b * cos)
        parts = fft_list(re, im, 1)
        zero = jnp.zeros((sub, LANES), F32)
        for part in range(2):
            y = parts[part]
            group = [jnp.where(lane < 96, y[a - 1] if a else zero, y[a] if a < count else zero) for a in range(count + 1)]
            group.append(zero)
            for u in range(count // 2):
                in_scr[u, part, span, :] = jnp.where(
                    lane < 64, y[2 * u], pltpu.roll(y[2 * u + 1], 64, 1)
                )
            for u in range(count // 2 + 1):
                out_scr[u, part, span, :] = jnp.where(
                    lane < 64, pltpu.roll(group[2 * u], 64, 1), group[2 * u + 1]
                )
    for k in range(devices):
        start = (me ^ k) * half
        at = 0
        for refs, tiles in zip(inner_refs[k], chunks):
            for t in range(tiles):
                refs[:, :, t * LANES : (t + 1) * LANES] = in_scr[start + at + t].astype(BF16)
            at += tiles
        for t in range(half + 1):
            outer_refs[k][:, :, t * LANES : (t + 1) * LANES] = out_scr[start + t].astype(BF16)
    if first[0] == 0:

        @pl.when(pl.program_id(0) == 0)
        def _():
            edge = edge_rows(slope_ref, centre_ref)
            wide = lax.broadcasted_iota(jnp.int32, (16, LANES), 1)
            for k in range(devices):
                at = slice(half * LANES, (half + 1) * LANES)
                known = outer_refs[k][0, :16, at].astype(F32)
                outer_refs[k][0, :16, at] = jnp.where(wide < 64, known, edge).astype(BF16)


def compress(echo, filt, slope, centre, valid, devices, part, parts, chunks, outer):
    _, rows, length = echo.shape
    count = length // LANES
    half = count // devices // 2
    mine = rows // parts
    step = min(64, mine)
    steps = mine // step
    natural = np.arange(LANES)
    turned = (natural + HALF) % LANES
    q = LANES // count
    freq = q * (natural % count) + natural // count
    twf = -angle_np(np.arange(count), natural, length)
    twi = angle_np(np.arange(count), turned, length)
    twiddles = np.stack([np.cos(twf), np.sin(twf), np.cos(twi), np.sin(twi)])
    mats = right_matrix(angle_np(natural, freq, LANES), -1) + right_matrix(
        angle_np(freq, turned, LANES), 1, 1.0 / length
    )
    inner_widths = [c * LANES for c in chunks] * devices
    width = (half + 1) * LANES
    outs = pl.pallas_call(
        functools.partial(
            range_kernel, devices=devices, first=(part * mine, rows), chunks=chunks, held=len(outer)
        ),
        grid=(steps,),
        in_specs=[
            pl.BlockSpec(memory_space=pltpu.SMEM),
            pl.BlockSpec((2, step, length), lambda i: (0, part * steps + i, 0)),
            pl.BlockSpec((2, length), lambda i: (0, 0)),
            pl.BlockSpec(slope.shape, lambda i: (0, 0)),
            pl.BlockSpec(slope.shape, lambda i: (0, 0)),
            pl.BlockSpec((4, count, LANES), lambda i: (0, 0, 0)),
            pl.BlockSpec((4, 2 * LANES, 2 * LANES), lambda i: (0, 0, 0)),
        ]
        + [pl.BlockSpec(memory_space=pl.ANY)] * len(outer),
        out_specs=[pl.BlockSpec((2, step, w), lambda i: (0, i, 0)) for w in inner_widths]
        + [pl.BlockSpec((2, step, width), lambda i: (0, part * steps + i, 0))] * devices,
        scratch_shapes=[
            pltpu.VMEM((count // 2, 2, step, LANES), F32),
            pltpu.VMEM((count // 2 + 1, 2, step, LANES), F32),
            pltpu.VMEM((2, count, LANES), F32),
        ],
        out_shape=[jax.ShapeDtypeStruct((2, mine, w), BF16) for w in inner_widths]
        + [jax.ShapeDtypeStruct((2, rows, width), BF16)] * devices,
        input_output_aliases={7 + k: len(inner_widths) + k for k in range(len(outer))},
        compiler_params=pltpu.CompilerParams(vmem_limit_bytes=RANGE_BYTES),
        cost_estimate=cost(9.0 / parts),
        name="range_compress",
    )(valid, echo, filt, slope, centre, jnp.asarray(twiddles, F32), jnp.asarray(np.stack(mats)), *outer)
    inner = [outs[k * len(chunks) : (k + 1) * len(chunks)] for k in range(devices)]
    return inner, outs[len(inner_widths) :]


def turn(turns):
    x = turns - jnp.round(turns)
    z = x * x
    a, b = [v * math.sqrt(2.0) for v in SIN_POLY], [v * math.sqrt(2.0) for v in COS_POLY]
    sin = x * (a[0] + z * (a[1] + z * (a[2] + z * a[3])))
    cos = b[0] + z * (b[1] + z * (b[2] + z * b[3]))
    return 1.0 - sin * sin, sin * cos


def focus_tile(scr, col, width, slope, centre, af_ref, ai_ref):
    lines = scr.shape[1]
    radix = lines // LANES
    at = slice(col, col + width)
    re = [scr[0, s * LANES : (s + 1) * LANES, at].astype(F32) for s in range(radix)]
    im = [scr[1, s * LANES : (s + 1) * LANES, at].astype(F32) for s in range(radix)]
    re, im = fft_list(re, im, -1)
    k = radix * lax.broadcasted_iota(jnp.int32, (LANES, width), 0)
    u = jnp.where(k >= lines // 2, k - lines, k).astype(F32) * (1.0 / lines)
    back_re, back_im = [], []
    rate = slope * (lines / 8.0)
    for c in range(radix):
        high, low = split(jnp.concatenate([re[c], im[c]], axis=0))
        freq = dot(af_ref[0, c], high) + dot(af_ref[0, c], low) + dot(af_ref[1, c], high)
        w = u - (centre - c / lines)
        cos, sin = turn(rate * w * w)
        a, b = freq[:LANES], freq[LANES:]
        high, low = split(jnp.concatenate([a * cos - b * sin, a * sin + b * cos], axis=0))
        back = dot(ai_ref[0, c], high) + dot(ai_ref[0, c], low) + dot(ai_ref[1, c], high)
        back_re.append(back[:LANES])
        back_im.append(back[LANES:])
    return fft_list(back_re, back_im, 1)


def azimuth_matrices(lines):
    radix = lines // LANES
    t = np.arange(LANES)
    forward, inverse = [], []
    for c in range(radix):
        k = c + radix * t
        forward.append(np.stack(left_matrix(angle_np(k, t, lines), -1)))
        inverse.append(np.stack(left_matrix(angle_np(t, k, lines), 1, 1.0 / lines)))
    return jnp.asarray(np.stack(forward, axis=1)), jnp.asarray(np.stack(inverse, axis=1))


def gather_lines(blocks, scr):
    me = lax.axis_index("lines")
    devices = len(blocks)
    rows = scr.shape[1] // devices
    for k, parts in enumerate(blocks):
        share = rows // len(parts)
        for h, part in enumerate(parts):
            start = pl.multiple_of((me ^ k) * rows + h * share, share)
            scr[:, pl.ds(start, share), :] = part[...]


def nested(refs, devices):
    per = len(refs) // devices
    return [refs[k * per : (k + 1) * per] for k in range(devices)]


def inner_kernel(*rest, devices, row_parts, parts):
    blocks, rest = nested(rest[: devices * row_parts], devices), rest[devices * row_parts :]
    slope_ref, centre_ref, af_ref, ai_ref, out_ref = rest[:5]
    p_refs, (scr, p_scr) = rest[5 : 5 + parts], rest[5 + parts :]
    gather_lines(blocks, scr)
    width = out_ref.shape[2]
    lane = lax.broadcasted_iota(jnp.int32, (1, LANES), 1)

    def packed(ref):
        tiles = []
        for t in range(width // LANES):
            a = pltpu.roll(ref[:, 2 * t * LANES : (2 * t + 1) * LANES], 96, 1)
            b = pltpu.roll(ref[:, (2 * t + 1) * LANES : (2 * t + 2) * LANES], 32, 1)
            tiles.append(jnp.where(lane < 64, a, b))
        return jnp.concatenate(tiles, axis=1)

    re, im = focus_tile(scr, 0, width, packed(slope_ref), packed(centre_ref), af_ref, ai_ref)
    for part, value in enumerate((re, im)):
        for s in range(len(value)):
            image = value[s].astype(BF16)
            out_ref[part, s * LANES : (s + 1) * LANES, :] = image
            p_scr[part, s * PATCH : (s + 1) * PATCH, :] = image[HALF : HALF + PATCH]
    share = p_scr.shape[1] // parts
    me = lax.axis_index("acq") if parts > 1 else 0
    for k in range(parts):
        start = pl.multiple_of((me ^ k) * share, share)
        p_refs[k][...] = p_scr[:, pl.ds(start, share), :]


def focus_inner(blocks, slope, centre, matrices, first, parts):
    devices, row_parts = len(blocks), len(blocks[0])
    _, rows, cols = blocks[0][0].shape
    lines = rows * devices * row_parts
    tile = 2 * LANES if cols % (2 * LANES) == 0 else LANES
    skip = first * LANES // (2 * tile)
    prows = lines // 2
    shape = (2, lines // LANES, 2 * LANES, 2 * LANES)
    return pl.pallas_call(
        functools.partial(inner_kernel, devices=devices, row_parts=row_parts, parts=parts),
        grid=(cols // tile,),
        in_specs=[pl.BlockSpec((2, rows, tile), lambda i: (0, 0, i))] * (devices * row_parts)
        + [pl.BlockSpec((1, 2 * tile), lambda i: (0, skip + i))] * 2
        + [pl.BlockSpec(shape, lambda i: (0, 0, 0, 0))] * 2,
        out_specs=[pl.BlockSpec((2, lines, tile), lambda i: (0, 0, i))]
        + [pl.BlockSpec((2, prows // parts, tile), lambda i: (0, 0, i))] * parts,
        scratch_shapes=[pltpu.VMEM((2, lines, tile), BF16), pltpu.VMEM((2, prows, tile), BF16)],
        out_shape=[jax.ShapeDtypeStruct((2, lines, cols), BF16)]
        + [jax.ShapeDtypeStruct((2, prows // parts, cols), BF16)] * parts,
        compiler_params=pltpu.CompilerParams(vmem_limit_bytes=VMEM_BYTES),
        cost_estimate=cost(0.8 * cols / LANES),
        name="focus_inner",
    )(*[part for parts_of in blocks for part in parts_of], slope, centre, *matrices)


def outer_kernel(*rest, devices):
    blocks, rest = rest[:devices], rest[devices:]
    slope_ref, centre_ref, af_ref, ai_ref, out_ref, scr = rest
    gather_lines([[b] for b in blocks], scr)
    width = scr.shape[2]
    lane = lax.broadcasted_iota(jnp.int32, (1, LANES), 1)
    pairs = width // LANES - 1

    me = lax.axis_index("lines")

    def extended(ref, row):
        before = after = jnp.zeros((1, LANES), F32)
        for k in range(1, devices):
            told = blocks[k][0, :16, pairs * LANES :].astype(F32)
            told = told[row : row + 1] + told[row + 1 : row + 2] + told[row + 2 : row + 3]
            before = jnp.where((me ^ k) == me - 1, told, before)
            after = jnp.where((me ^ k) == me + 1, pltpu.roll(told, 64, 1), after)
        return [before] + [ref[:, t * LANES : (t + 1) * LANES] for t in range(ref.shape[1] // LANES)] + [after]

    def group(values, a):
        return jnp.where(lane < 96, pltpu.roll(values[a], 96, 1), pltpu.roll(values[a + 1], 96, 1))

    def packed(values, u):
        left = pltpu.roll(group(values, 2 * u), 64, 1)
        if u == pairs:
            return jnp.where(lane < 64, left, 0.0)
        return jnp.where(lane < 64, left, group(values, 2 * u + 1))

    slopes, centres = extended(slope_ref, 0), extended(centre_ref, 3)
    u = 0
    while u <= pairs:
        tiles = min(2, pairs + 1 - u)
        slope = jnp.concatenate([packed(slopes, u + t) for t in range(tiles)], axis=1)
        centre = jnp.concatenate([packed(centres, u + t) for t in range(tiles)], axis=1)
        at = slice(u * LANES, (u + tiles) * LANES)
        for part, value in enumerate(focus_tile(scr, u * LANES, tiles * LANES, slope, centre, af_ref, ai_ref)):
            for s in range(len(value)):
                out_ref[part, s * LANES : (s + 1) * LANES, at] = value[s].astype(BF16)
        u += tiles


def focus_outer(blocks, slope, centre, matrices):
    devices = len(blocks)
    _, rows, cols = blocks[0].shape
    lines = rows * devices
    vmem = pl.BlockSpec(memory_space=pltpu.VMEM)
    return pl.pallas_call(
        functools.partial(outer_kernel, devices=devices),
        in_specs=[vmem] * (devices + 4),
        out_specs=vmem,
        out_shape=jax.ShapeDtypeStruct((2, lines, cols), BF16),
        scratch_shapes=[pltpu.VMEM((2, lines, cols), BF16)],
        compiler_params=pltpu.CompilerParams(vmem_limit_bytes=VMEM_BYTES),
        cost_estimate=cost(4.0),
        name="focus_outer",
    )(*blocks, slope, centre, *matrices)


def patch_matrices():
    n = np.arange(PATCH)
    theta = angle_np(n, n, PATCH)

    def lanes(sign):
        cos = np.kron(np.eye(2), np.cos(theta))
        sin = sign * np.kron(np.eye(2), np.sin(theta))
        return np.stack(split_np(np.block([[cos, sin], [-sin, cos]])))

    high, low = split_np(np.concatenate([np.cos(theta), np.sin(theta)], axis=0))
    column = np.concatenate([high, high, low], axis=1)
    return jnp.asarray(lanes(-1)), jnp.asarray(lanes(1)), jnp.asarray(column)


def columns(value, column_ref, sign):
    high, low = split(value)
    both = dot(column_ref[...], jnp.concatenate([high, low, high], axis=0))
    c_re, c_im = both[:PATCH, :LANES], both[:PATCH, LANES:]
    s_re, s_im = both[PATCH:, :LANES], both[PATCH:, LANES:]
    if sign < 0:
        return c_re + s_im, c_im - s_re
    return c_re - s_im, c_im + s_re


def power(re, im):
    lane = lax.broadcasted_iota(jnp.int32, (1, LANES), 1)
    total = jnp.sum(re * re + im * im, axis=0, keepdims=True)
    left = jnp.sum(jnp.where(lane < PATCH, total, 0.0), axis=1, keepdims=True)
    right = jnp.sum(jnp.where(lane < PATCH, 0.0, total), axis=1, keepdims=True)
    return jnp.where(lane < PATCH, left, right) * (1.0 / (PATCH * PATCH))


def window_kernel(offsets, *rest, chunks):
    inner_refs, rest = rest[: len(chunks)], rest[len(chunks) :]
    outer_ref, lane_ref, column_ref = rest[:3]
    spec_ref, image, windows = rest[3:]
    lines, pairs = outer_ref.shape[1], outer_ref.shape[2] // LANES - 1
    lane = lax.broadcasted_iota(jnp.int32, (1, LANES), 1)
    edge = jnp.zeros((HALF, image.shape[2]), F32)
    for part in range(2):
        image[part, :HALF, :] = edge
        image[part, HALF + lines : 2 * HALF + lines, :] = edge
    where = [(c, t) for c, tiles in enumerate(chunks) for t in range(tiles)]
    for u in range(pairs + 1):
        for part in range(2):
            fresh = outer_ref[part, :, u * LANES : (u + 1) * LANES].astype(F32)
            at = slice(HALF, HALF + lines)
            if u == pairs:
                image[part, at, 2 * u * LANES : (2 * u + 1) * LANES] = fresh
                continue
            c, t = where[u]
            known = inner_refs[c][part, :, t * LANES : (t + 1) * LANES].astype(F32)
            image[part, at, 2 * u * LANES : (2 * u + 1) * LANES] = jnp.where(
                lane < 64, fresh, pltpu.roll(known, 64, 1)
            )
            image[part, at, (2 * u + 1) * LANES : (2 * u + 2) * LANES] = jnp.where(
                lane < 64, pltpu.roll(fresh, 64, 1), known
            )
    row_blocks = lines // (2 * PATCH)
    wide = lax.broadcasted_iota(jnp.int32, (PATCH + 8, LANES), 1)

    def block(i, carry):
        gains = []
        for u in range(pairs):
            found = [[], []]
            for side in range(2):
                j = 2 * u + side
                start = 2 * PATCH * i + PATCH + offsets[0, i, j]
                shift = PATCH + offsets[1, i, j]
                back = jnp.bitwise_and(2 * LANES - shift + side * PATCH, LANES - 1)
                base = pl.multiple_of(lax.shift_left(lax.shift_right_logical(start, 3), 3), 8)
                up = PATCH + 8 - jnp.bitwise_and(start, 7)
                for part in range(2):
                    left = image[part, pl.ds(base, PATCH + 8), j * LANES : (j + 1) * LANES]
                    right = image[part, pl.ds(base, PATCH + 8), (j + 1) * LANES : (j + 2) * LANES]
                    turned = pltpu.roll(jnp.where(wide >= shift, left, right), back, 1)
                    found[part].append(pltpu.roll(turned, up, 0)[:PATCH])
            re = jnp.where(lane < PATCH, found[0][0], found[0][1])
            im = jnp.where(lane < PATCH, found[1][0], found[1][1])
            gains.append(lax.rsqrt(power(re, im) + EPS) * (1.0 / PATCH**3))
            windows[u * PATCH : (u + 1) * PATCH, :] = jnp.concatenate([re, im], axis=1).astype(BF16)
        mixed = dot(windows[...], lane_ref[0]) + dot(windows[...], lane_ref[1])
        for u in range(pairs):
            re, im = columns(mixed[u * PATCH : (u + 1) * PATCH], column_ref, -1)
            spec_ref[0, i * pairs + u] = re * gains[u]
            spec_ref[1, i * pairs + u] = im * gains[u]
        return carry

    lax.fori_loop(0, row_blocks, block, 0)


def window_spectra(inner, outer, patch, offsets, chunks):
    lines, pairs = outer.shape[1], outer.shape[2] // LANES - 1
    vmem = pl.BlockSpec(memory_space=pltpu.VMEM)
    return pl.pallas_call(
        functools.partial(window_kernel, chunks=chunks),
        in_specs=[pl.BlockSpec(memory_space=pltpu.SMEM)] + [vmem] * (len(chunks) + 3),
        out_specs=vmem,
        out_shape=jax.ShapeDtypeStruct((2, lines // (2 * PATCH) * pairs, PATCH, LANES), F32),
        scratch_shapes=[
            pltpu.VMEM((2, lines + 2 * HALF + 8, (2 * pairs + 1) * LANES), F32),
            pltpu.VMEM((pairs * PATCH, 2 * LANES), BF16),
        ],
        compiler_params=pltpu.CompilerParams(vmem_limit_bytes=VMEM_BYTES),
        cost_estimate=cost(4.0),
        name="window_spectra",
    )(offsets, *inner, outer, patch[0], patch[2])


def primary_kernel(reference, *rest, parts):
    shares, (lane_ref, column_ref, out_ref, scr) = rest[:-4], rest[-4:]
    source = lax.axis_index("acq") ^ reference[0] if parts > 1 else 0
    for k in range(parts):

        @pl.when(source == k)
        def _(k=k):
            col = 0
            for ref in shares[k::parts]:
                scr[:, :, col : col + ref.shape[2]] = ref[...]
                col += ref.shape[2]

    rows, cols = scr.shape[1], scr.shape[2]
    for u in range(cols // LANES):
        lanes = slice(u * LANES, (u + 1) * LANES)
        both = jnp.concatenate([scr[0, :, lanes], scr[1, :, lanes]], axis=1)
        mixed = dot(both, lane_ref[0]) + dot(both, lane_ref[1])
        for i in range(rows // PATCH):
            at = slice(i * PATCH, (i + 1) * PATCH)
            value = both[at].astype(F32)
            gain = lax.rsqrt(power(value[:, :LANES], value[:, LANES:]) + EPS)
            re, im = columns(mixed[at], column_ref, -1)
            out_ref[0, at, lanes] = (re * gain).astype(BF16)
            out_ref[1, at, lanes] = (im * gain).astype(BF16)


def primary_spectra(reference, shares, patch):
    vmem = pl.BlockSpec(memory_space=pltpu.VMEM)
    flat = [share for chunk in shares for share in chunk]
    shape = flat[0].shape[:2] + (sum(chunk[0].shape[2] for chunk in shares),)
    return pl.pallas_call(
        functools.partial(primary_kernel, parts=len(shares[0])),
        in_specs=[pl.BlockSpec(memory_space=pltpu.SMEM)] + [vmem] * (len(flat) + 2),
        out_specs=vmem,
        out_shape=jax.ShapeDtypeStruct(shape, BF16),
        scratch_shapes=[pltpu.VMEM(shape, BF16)],
        compiler_params=pltpu.CompilerParams(vmem_limit_bytes=VMEM_BYTES),
        cost_estimate=cost(1.0),
        name="primary_spectra",
    )(reference, *flat, patch[0], patch[2])


def correlate_kernel(*rest, parts):
    shares, (spec_ref, inverse_ref, column_ref, out_ref) = rest[:parts], rest[parts:]
    _, rows, cols = shares[0].shape
    pairs = cols // LANES
    per = rows // PATCH
    me = lax.axis_index("acq") if parts > 1 else 0
    for k in range(parts):
        for r in range(per):
            i = (me ^ k) * per + r
            middle = []
            for u in range(pairs):
                at, lanes = slice(r * PATCH, (r + 1) * PATCH), slice(u * LANES, (u + 1) * LANES)
                p_re, p_im = shares[k][0, at, lanes].astype(F32), shares[k][1, at, lanes].astype(F32)
                s_re, s_im = spec_ref[0, i * pairs + u], spec_ref[1, i * pairs + u]
                cross = jnp.concatenate([p_re * s_re + p_im * s_im, p_im * s_re - p_re * s_im], axis=1)
                middle.append(jnp.concatenate(columns(cross, column_ref, 1), axis=1))
            surface = three_pass(split(jnp.concatenate(middle, axis=0)), inverse_ref[0], inverse_ref[1])
            line = pl.ds(pl.multiple_of(i * PATCH, PATCH), PATCH)
            for u in range(pairs):
                lanes = slice(u * LANES, (u + 1) * LANES)
                block = surface[u * PATCH : (u + 1) * PATCH]
                out_ref[0, 0, line, lanes] = block[:, :LANES]
                out_ref[0, 1, line, lanes] = block[:, LANES:]


def correlate(shares, spectrum, patch):
    parts = len(shares)
    _, rows, cols = shares[0].shape
    vmem = pl.BlockSpec(memory_space=pltpu.VMEM)
    return pl.pallas_call(
        functools.partial(correlate_kernel, parts=parts),
        in_specs=[vmem] * (parts + 3),
        out_specs=vmem,
        out_shape=jax.ShapeDtypeStruct((1, 2, rows * parts, cols), F32),
        compiler_params=pltpu.CompilerParams(vmem_limit_bytes=VMEM_BYTES),
        cost_estimate=cost(2.0),
        name="correlate",
    )(*shares, spectrum, patch[1], patch[2])


def far_first(devices):
    return list(range(2, devices)) + list(range(min(2, devices)))[::-1]


def trade(block, k, axis):
    if k == 0:
        return block
    return lax.ppermute(block, axis, [(i, i ^ k) for i in range(lax.axis_size(axis))])


def on_device(echo, filt, slope, centre, valid, reference, offsets):
    devices, parts = lax.axis_size("lines"), lax.axis_size("acq")
    rows, length = echo.shape[2], echo.shape[3]
    lines = rows * devices
    tiles = length // devices // (2 * LANES)
    chunks = (tiles // COLUMN_PARTS,) * COLUMN_PARTS if tiles % COLUMN_PARTS == 0 else (tiles,)
    row_parts = ROW_PARTS if rows % (32 * ROW_PARTS) == 0 else 1
    spread = lines // (2 * PATCH) % parts == 0
    matrices = azimuth_matrices(lines)
    patch = patch_matrices()
    inner = [[[] for _ in range(devices)] for _ in chunks]
    outer = []
    for h in range(row_parts):
        mine, outer = compress(echo[0], filt[0], slope, centre, valid, devices, h, row_parts, chunks, outer)
        for c in range(len(chunks)):
            for k in far_first(devices):
                inner[c][k].append(trade(mine[k][c], k, "lines"))
    near = trade(outer[1], 1, "lines")
    if len(inner) > 1:
        inner[-1], near = lax.optimization_barrier((inner[-1], near))
    images, primaries = [], []
    for c in range(len(chunks)):
        image, *shares = focus_inner(
            inner[c], slope, centre, matrices, 2 * sum(chunks[:c]), parts if spread else 1
        )
        images.append(image)
        if spread:
            shares = {k: trade(shares[k], k, "acq") for k in far_first(parts)}
            shares = [shares[k] for k in range(parts)]
        else:
            mine = lax.axis_index("acq") == reference[0]
            shares = [lax.psum(jnp.where(mine, shares[0], 0).astype(BF16), "acq")]
        primaries.append(shares)
    far, _ = lax.optimization_barrier((list(outer[2:]), images[0]))
    far = [trade(block, k + 2, "lines") for k, block in enumerate(far)]
    outer = [outer[0], near, *far]
    outer = focus_outer(outer, slope, centre, matrices)
    spectrum = window_spectra(images, outer, patch, offsets[0], chunks)
    shares = [primary_spectra(reference, primaries, patch)]
    for k in range(1, parts if spread else 1):
        low = k & -k
        shares.append(trade(shares[k - low], low, "acq"))
    return correlate(shares, spectrum, patch)


def solution(mesh):
    return jax.shard_map(
        on_device,
        mesh=mesh,
        in_specs=(
            P(("stack", "acq"), None, "lines", None),
            P(("stack", "acq"), None, None),
            P(("stack", "acq"), "lines"),
            P(("stack", "acq"), "lines"),
            P(("stack", "acq")),
            P("stack"),
            P(("stack", "acq"), None, None, "lines"),
        ),
        out_specs=P(("stack", "acq"), None, None, "lines"),
        check_vma=False,
    )
```

```python
import functools
import math

import jax
import jax.numpy as jnp
import ml_dtypes
import numpy as np
from jax import lax
from jax.experimental import pallas as pl
from jax.experimental.pallas import tpu as pltpu
from jax.sharding import PartitionSpec as P

PATCH = 64
LANES = 128
HALF = PATCH // 2
EPS = 1e-06
F32 = jnp.float32
BF16 = jnp.bfloat16
VMEM_BYTES = 32 * 1024 * 1024
RANGE_BYTES = 60 * 1024 * 1024

ROW_PARTS = 1
COLUMN_PARTS = 2

SIN_POLY = (3.141582022139052, -5.167142795074894, 2.541899011376644, -0.5546361478584824)
COS_POLY = (0.9999933027022169, -4.9339382503784215, 4.041285686469419, -1.2221312612719153)


def split_np(matrix):
    high = matrix.astype(ml_dtypes.bfloat16)
    low = (matrix - high.astype(np.float64)).astype(ml_dtypes.bfloat16)
    return high, low


def angle_np(rows, cols, period):
    return 2.0 * np.pi * ((np.asarray(rows)[:, None] * np.asarray(cols)[None, :]) % period) / period


def right_matrix(theta, sign, scale=1.0):
    cos, sin = np.cos(theta) * scale, sign * np.sin(theta) * scale
    return split_np(np.block([[cos, sin], [-sin, cos]]))


def left_matrix(theta, sign, scale=1.0):
    cos, sin = np.cos(theta) * scale, sign * np.sin(theta) * scale
    return split_np(np.block([[cos, -sin], [sin, cos]]))


def cost(microseconds):
    return pl.CostEstimate(
        flops=int(microseconds * 1e9), bytes_accessed=int(microseconds * 3.5e6), transcendentals=0
    )


def split(value):
    high = value.astype(BF16)
    low = (value - high.astype(F32)).astype(BF16)
    return high, low


def dot(lhs, rhs):
    return jnp.dot(lhs, rhs, preferred_element_type=F32)


def fft_list(re, im, sign):
    size = len(re)
    if size == 1:
        return re, im
    if size == 2:
        return [re[0] + re[1], re[0] - re[1]], [im[0] + im[1], im[0] - im[1]]
    even_re, even_im = fft_list(re[0::2], im[0::2], sign)
    odd_re, odd_im = fft_list(re[1::2], im[1::2], sign)
    half = size // 2
    out_re, out_im = [None] * size, [None] * size
    root = math.sqrt(0.5)
    for k in range(half):
        a, b = odd_re[k], odd_im[k]
        if k == 0:
            t_re, t_im = a, b
        elif 4 * k == size:
            t_re, t_im = (b, -a) if sign < 0 else (-b, a)
        elif 8 * k == size:
            t_re, t_im = ((a + b) * root, (b - a) * root) if sign < 0 else ((a - b) * root, (a + b) * root)
        elif 8 * k == 3 * size:
            t_re, t_im = ((b - a) * root, (a + b) * -root) if sign < 0 else ((a + b) * -root, (a - b) * root)
        else:
            cos = math.cos(2.0 * math.pi * k / size)
            sin = sign * math.sin(2.0 * math.pi * k / size)
            t_re, t_im = a * cos - b * sin, a * sin + b * cos
        if 4 * k == size:
            if sign < 0:
                out_re[k], out_re[k + half] = even_re[k] + b, even_re[k] - b
                out_im[k], out_im[k + half] = even_im[k] - a, even_im[k] + a
            else:
                out_re[k], out_re[k + half] = even_re[k] - b, even_re[k] + b
                out_im[k], out_im[k + half] = even_im[k] + a, even_im[k] - a
            continue
        out_re[k], out_re[k + half] = even_re[k] + t_re, even_re[k] - t_re
        out_im[k], out_im[k + half] = even_im[k] + t_im, even_im[k] - t_im
    return out_re, out_im


def three_pass(lhs, high, low):
    lhs_high, lhs_low = lhs
    return dot(lhs_high, high) + dot(lhs_low, high) + dot(lhs_high, low)


def spread_filter(filt_ref, out):
    count = out.shape[1]
    for part in range(2):
        rows = [filt_ref[part : part + 1, a * LANES : (a + 1) * LANES] for a in range(count)]
        rows.append(jnp.zeros((LANES - count, LANES), F32))
        turned = jnp.concatenate(rows, axis=0).T
        out[part] = jnp.concatenate(
            [turned[e * count : (e + 1) * count, :count] for e in range(LANES // count)], axis=1
        )


def edge_rows(slope_ref, centre_ref):
    lane = lax.broadcasted_iota(jnp.int32, (1, LANES), 1)
    rows = []
    for ref in (slope_ref, centre_ref):
        value = jnp.where(lane < 96, pltpu.roll(ref[:, :LANES], 64, 1), ref[:, -LANES:])
        for _ in range(3):
            part = value.astype(BF16).astype(F32)
            rows.append(part)
            value = value - part
    return jnp.concatenate(rows + [jnp.zeros((16 - len(rows), LANES), F32)], axis=0)


def range_kernel(valid, x_ref, filter_ref, slope_ref, centre_ref, tw_ref, mat_ref, *rest, devices, first, chunks, held):
    rest = rest[held:]
    outs, (in_scr, out_scr, filt_ref) = rest[:-3], rest[-3:]
    inner_refs = [outs[k * len(chunks) : (k + 1) * len(chunks)] for k in range(devices)]
    outer_refs = outs[devices * len(chunks) :]
    rows, length = x_ref.shape[1], x_ref.shape[2]
    count = length // LANES
    half = count // devices // 2
    me = lax.axis_index("lines")
    sub = 8

    @pl.when(pl.program_id(0) == 0)
    def _():
        spread_filter(filter_ref, filt_ref)

    base = me * first[1] + first[0] + pl.program_id(0) * rows
    lane = lax.broadcasted_iota(jnp.int32, (sub, LANES), 1)
    for block in range(rows // sub):
        span = slice(block * sub, (block + 1) * sub)
        odd = block * sub % 16
        whole = slice(block * sub - odd, block * sub - odd + 16)
        keep = base + block * sub + lax.broadcasted_iota(jnp.int32, (sub, LANES), 0) < valid[0]
        re, im = [], []
        for a in range(count):
            at = slice(a * LANES, (a + 1) * LANES)
            re.append(jnp.where(keep, x_ref[0, whole, at].astype(F32)[odd : odd + sub], 0.0))
            im.append(jnp.where(keep, x_ref[1, whole, at].astype(F32)[odd : odd + sub], 0.0))
        re, im = fft_list(re, im, -1)
        mixed = []
        for c in range(count):
            cos, sin = tw_ref[0, c : c + 1, :], tw_ref[1, c : c + 1, :]
            mixed.append(jnp.concatenate([re[c] * cos - im[c] * sin, re[c] * sin + im[c] * cos], axis=1))
        spectrum = three_pass(split(jnp.concatenate(mixed, 0)), mat_ref[0], mat_ref[1])
        mixed = []
        for c in range(count):
            at = slice(c * sub, (c + 1) * sub)
            a, b = spectrum[at, :LANES], spectrum[at, LANES:]
            cos, sin = filt_ref[0, c : c + 1, :], filt_ref[1, c : c + 1, :]
            mixed.append(jnp.concatenate([a * cos - b * sin, a * sin + b * cos], axis=1))
        pulse = three_pass(split(jnp.concatenate(mixed, 0)), mat_ref[2], mat_ref[3])
        re, im = [], []
        for c in range(count):
            at = slice(c * sub, (c + 1) * sub)
            a, b = pulse[at, :LANES], pulse[at, LANES:]
            cos, sin = tw_ref[2, c : c + 1, :], tw_ref[3, c : c + 1, :]
            re.append(a * cos - b * sin)
            im.append(a * sin + b * cos)
        parts = fft_list(re, im, 1)
        zero = jnp.zeros((sub, LANES), F32)
        for part in range(2):
            y = parts[part]
            group = [jnp.where(lane < 96, y[a - 1] if a else zero, y[a] if a < count else zero) for a in range(count + 1)]
            group.append(zero)
            for u in range(count // 2):
                in_scr[u, part, span, :] = jnp.where(
                    lane < 64, y[2 * u], pltpu.roll(y[2 * u + 1], 64, 1)
                )
            for u in range(count // 2 + 1):
                out_scr[u, part, span, :] = jnp.where(
                    lane < 64, pltpu.roll(group[2 * u], 64, 1), group[2 * u + 1]
                )
    for k in range(devices):
        start = (me ^ k) * half
        at = 0
        for refs, tiles in zip(inner_refs[k], chunks):
            for t in range(tiles):
                refs[:, :, t * LANES : (t + 1) * LANES] = in_scr[start + at + t].astype(BF16)
            at += tiles
        for t in range(half + 1):
            outer_refs[k][:, :, t * LANES : (t + 1) * LANES] = out_scr[start + t].astype(BF16)
    if first[0] == 0:

        @pl.when(pl.program_id(0) == 0)
        def _():
            edge = edge_rows(slope_ref, centre_ref)
            wide = lax.broadcasted_iota(jnp.int32, (16, LANES), 1)
            for k in range(devices):
                at = slice(half * LANES, (half + 1) * LANES)
                known = outer_refs[k][0, :16, at].astype(F32)
                outer_refs[k][0, :16, at] = jnp.where(wide < 64, known, edge).astype(BF16)


def compress(echo, filt, slope, centre, valid, devices, part, parts, chunks, outer):
    _, rows, length = echo.shape
    count = length // LANES
    half = count // devices // 2
    mine = rows // parts
    step = min(64, mine)
    steps = mine // step
    natural = np.arange(LANES)
    turned = (natural + HALF) % LANES
    q = LANES // count
    freq = q * (natural % count) + natural // count
    twf = -angle_np(np.arange(count), natural, length)
    twi = angle_np(np.arange(count), turned, length)
    twiddles = np.stack([np.cos(twf), np.sin(twf), np.cos(twi), np.sin(twi)])
    mats = right_matrix(angle_np(natural, freq, LANES), -1) + right_matrix(
        angle_np(freq, turned, LANES), 1, 1.0 / length
    )
    inner_widths = [c * LANES for c in chunks] * devices
    width = (half + 1) * LANES
    outs = pl.pallas_call(
        functools.partial(
            range_kernel, devices=devices, first=(part * mine, rows), chunks=chunks, held=len(outer)
        ),
        grid=(steps,),
        in_specs=[
            pl.BlockSpec(memory_space=pltpu.SMEM),
            pl.BlockSpec((2, step, length), lambda i: (0, part * steps + i, 0)),
            pl.BlockSpec((2, length), lambda i: (0, 0)),
            pl.BlockSpec(slope.shape, lambda i: (0, 0)),
            pl.BlockSpec(slope.shape, lambda i: (0, 0)),
            pl.BlockSpec((4, count, LANES), lambda i: (0, 0, 0)),
            pl.BlockSpec((4, 2 * LANES, 2 * LANES), lambda i: (0, 0, 0)),
        ]
        + [pl.BlockSpec(memory_space=pl.ANY)] * len(outer),
        out_specs=[pl.BlockSpec((2, step, w), lambda i: (0, i, 0)) for w in inner_widths]
        + [pl.BlockSpec((2, step, width), lambda i: (0, part * steps + i, 0))] * devices,
        scratch_shapes=[
            pltpu.VMEM((count // 2, 2, step, LANES), F32),
            pltpu.VMEM((count // 2 + 1, 2, step, LANES), F32),
            pltpu.VMEM((2, count, LANES), F32),
        ],
        out_shape=[jax.ShapeDtypeStruct((2, mine, w), BF16) for w in inner_widths]
        + [jax.ShapeDtypeStruct((2, rows, width), BF16)] * devices,
        input_output_aliases={7 + k: len(inner_widths) + k for k in range(len(outer))},
        compiler_params=pltpu.CompilerParams(vmem_limit_bytes=RANGE_BYTES),
        cost_estimate=cost(9.0 / parts),
        name="range_compress",
    )(valid, echo, filt, slope, centre, jnp.asarray(twiddles, F32), jnp.asarray(np.stack(mats)), *outer)
    inner = [outs[k * len(chunks) : (k + 1) * len(chunks)] for k in range(devices)]
    return inner, outs[len(inner_widths) :]


def turn(turns):
    x = turns - jnp.round(turns)
    z = x * x
    a, b = [v * math.sqrt(2.0) for v in SIN_POLY], [v * math.sqrt(2.0) for v in COS_POLY]
    sin = x * (a[0] + z * (a[1] + z * (a[2] + z * a[3])))
    cos = b[0] + z * (b[1] + z * (b[2] + z * b[3]))
    return 1.0 - sin * sin, sin * cos


def focus_tile(scr, col, width, slope, centre, af_ref, ai_ref):
    lines = scr.shape[1]
    radix = lines // LANES
    at = slice(col, col + width)
    re = [scr[0, s * LANES : (s + 1) * LANES, at].astype(F32) for s in range(radix)]
    im = [scr[1, s * LANES : (s + 1) * LANES, at].astype(F32) for s in range(radix)]
    re, im = fft_list(re, im, -1)
    k = radix * lax.broadcasted_iota(jnp.int32, (LANES, width), 0)
    u = jnp.where(k >= lines // 2, k - lines, k).astype(F32) * (1.0 / lines)
    back_re, back_im = [], []
    rate = slope * (lines / 8.0)
    for c in range(radix):
        high, low = split(jnp.concatenate([re[c], im[c]], axis=0))
        freq = dot(af_ref[0, c], high) + dot(af_ref[0, c], low) + dot(af_ref[1, c], high)
        w = u - (centre - c / lines)
        cos, sin = turn(rate * w * w)
        a, b = freq[:LANES], freq[LANES:]
        high, low = split(jnp.concatenate([a * cos - b * sin, a * sin + b * cos], axis=0))
        back = dot(ai_ref[0, c], high) + dot(ai_ref[0, c], low) + dot(ai_ref[1, c], high)
        back_re.append(back[:LANES])
        back_im.append(back[LANES:])
    return fft_list(back_re, back_im, 1)


def azimuth_matrices(lines):
    radix = lines // LANES
    t = np.arange(LANES)
    forward, inverse = [], []
    for c in range(radix):
        k = c + radix * t
        forward.append(np.stack(left_matrix(angle_np(k, t, lines), -1)))
        inverse.append(np.stack(left_matrix(angle_np(t, k, lines), 1, 1.0 / lines)))
    return jnp.asarray(np.stack(forward, axis=1)), jnp.asarray(np.stack(inverse, axis=1))


def gather_lines(blocks, scr):
    me = lax.axis_index("lines")
    devices = len(blocks)
    rows = scr.shape[1] // devices
    for k, parts in enumerate(blocks):
        share = rows // len(parts)
        for h, part in enumerate(parts):
            start = pl.multiple_of((me ^ k) * rows + h * share, share)
            scr[:, pl.ds(start, share), :] = part[...]


def nested(refs, devices):
    per = len(refs) // devices
    return [refs[k * per : (k + 1) * per] for k in range(devices)]


def inner_kernel(*rest, devices, row_parts, parts):
    blocks, rest = nested(rest[: devices * row_parts], devices), rest[devices * row_parts :]
    slope_ref, centre_ref, af_ref, ai_ref, out_ref = rest[:5]
    p_refs, (scr, p_scr) = rest[5 : 5 + parts], rest[5 + parts :]
    gather_lines(blocks, scr)
    width = out_ref.shape[2]
    lane = lax.broadcasted_iota(jnp.int32, (1, LANES), 1)

    def packed(ref):
        tiles = []
        for t in range(width // LANES):
            a = pltpu.roll(ref[:, 2 * t * LANES : (2 * t + 1) * LANES], 96, 1)
            b = pltpu.roll(ref[:, (2 * t + 1) * LANES : (2 * t + 2) * LANES], 32, 1)
            tiles.append(jnp.where(lane < 64, a, b))
        return jnp.concatenate(tiles, axis=1)

    re, im = focus_tile(scr, 0, width, packed(slope_ref), packed(centre_ref), af_ref, ai_ref)
    for part, value in enumerate((re, im)):
        for s in range(len(value)):
            image = value[s].astype(BF16)
            out_ref[part, s * LANES : (s + 1) * LANES, :] = image
            p_scr[part, s * PATCH : (s + 1) * PATCH, :] = image[HALF : HALF + PATCH]
    share = p_scr.shape[1] // parts
    me = lax.axis_index("acq") if parts > 1 else 0
    for k in range(parts):
        start = pl.multiple_of((me ^ k) * share, share)
        p_refs[k][...] = p_scr[:, pl.ds(start, share), :]


def focus_inner(blocks, slope, centre, matrices, first, parts):
    devices, row_parts = len(blocks), len(blocks[0])
    _, rows, cols = blocks[0][0].shape
    lines = rows * devices * row_parts
    tile = 2 * LANES if cols % (2 * LANES) == 0 else LANES
    skip = first * LANES // (2 * tile)
    prows = lines // 2
    shape = (2, lines // LANES, 2 * LANES, 2 * LANES)
    return pl.pallas_call(
        functools.partial(inner_kernel, devices=devices, row_parts=row_parts, parts=parts),
        grid=(cols // tile,),
        in_specs=[pl.BlockSpec((2, rows, tile), lambda i: (0, 0, i))] * (devices * row_parts)
        + [pl.BlockSpec((1, 2 * tile), lambda i: (0, skip + i))] * 2
        + [pl.BlockSpec(shape, lambda i: (0, 0, 0, 0))] * 2,
        out_specs=[pl.BlockSpec((2, lines, tile), lambda i: (0, 0, i))]
        + [pl.BlockSpec((2, prows // parts, tile), lambda i: (0, 0, i))] * parts,
        scratch_shapes=[pltpu.VMEM((2, lines, tile), BF16), pltpu.VMEM((2, prows, tile), BF16)],
        out_shape=[jax.ShapeDtypeStruct((2, lines, cols), BF16)]
        + [jax.ShapeDtypeStruct((2, prows // parts, cols), BF16)] * parts,
        compiler_params=pltpu.CompilerParams(vmem_limit_bytes=VMEM_BYTES),
        cost_estimate=cost(0.8 * cols / LANES),
        name="focus_inner",
    )(*[part for parts_of in blocks for part in parts_of], slope, centre, *matrices)


def outer_kernel(*rest, devices):
    blocks, rest = rest[:devices], rest[devices:]
    slope_ref, centre_ref, af_ref, ai_ref, out_ref, scr = rest
    gather_lines([[b] for b in blocks], scr)
    width = scr.shape[2]
    lane = lax.broadcasted_iota(jnp.int32, (1, LANES), 1)
    pairs = width // LANES - 1

    me = lax.axis_index("lines")

    def extended(ref, row):
        before = after = jnp.zeros((1, LANES), F32)
        for k in range(1, devices):
            told = blocks[k][0, :16, pairs * LANES :].astype(F32)
            told = told[row : row + 1] + told[row + 1 : row + 2] + told[row + 2 : row + 3]
            before = jnp.where((me ^ k) == me - 1, told, before)
            after = jnp.where((me ^ k) == me + 1, pltpu.roll(told, 64, 1), after)
        return [before] + [ref[:, t * LANES : (t + 1) * LANES] for t in range(ref.shape[1] // LANES)] + [after]

    def group(values, a):
        return jnp.where(lane < 96, pltpu.roll(values[a], 96, 1), pltpu.roll(values[a + 1], 96, 1))

    def packed(values, u):
        left = pltpu.roll(group(values, 2 * u), 64, 1)
        if u == pairs:
            return jnp.where(lane < 64, left, 0.0)
        return jnp.where(lane < 64, left, group(values, 2 * u + 1))

    slopes, centres = extended(slope_ref, 0), extended(centre_ref, 3)
    u = 0
    while u <= pairs:
        tiles = min(2, pairs + 1 - u)
        slope = jnp.concatenate([packed(slopes, u + t) for t in range(tiles)], axis=1)
        centre = jnp.concatenate([packed(centres, u + t) for t in range(tiles)], axis=1)
        at = slice(u * LANES, (u + tiles) * LANES)
        for part, value in enumerate(focus_tile(scr, u * LANES, tiles * LANES, slope, centre, af_ref, ai_ref)):
            for s in range(len(value)):
                out_ref[part, s * LANES : (s + 1) * LANES, at] = value[s].astype(BF16)
        u += tiles


def focus_outer(blocks, slope, centre, matrices):
    devices = len(blocks)
    _, rows, cols = blocks[0].shape
    lines = rows * devices
    vmem = pl.BlockSpec(memory_space=pltpu.VMEM)
    return pl.pallas_call(
        functools.partial(outer_kernel, devices=devices),
        in_specs=[vmem] * (devices + 4),
        out_specs=vmem,
        out_shape=jax.ShapeDtypeStruct((2, lines, cols), BF16),
        scratch_shapes=[pltpu.VMEM((2, lines, cols), BF16)],
        compiler_params=pltpu.CompilerParams(vmem_limit_bytes=VMEM_BYTES),
        cost_estimate=cost(4.0),
        name="focus_outer",
    )(*blocks, slope, centre, *matrices)


def patch_matrices():
    n = np.arange(PATCH)
    theta = angle_np(n, n, PATCH)

    def lanes(sign):
        cos = np.kron(np.eye(2), np.cos(theta))
        sin = sign * np.kron(np.eye(2), np.sin(theta))
        return np.stack(split_np(np.block([[cos, sin], [-sin, cos]])))

    high, low = split_np(np.concatenate([np.cos(theta), np.sin(theta)], axis=0))
    column = np.concatenate([high, high, low], axis=1)
    return jnp.asarray(lanes(-1)), jnp.asarray(lanes(1)), jnp.asarray(column)


def columns(value, column_ref, sign):
    high, low = split(value)
    both = dot(column_ref[...], jnp.concatenate([high, low, high], axis=0))
    c_re, c_im = both[:PATCH, :LANES], both[:PATCH, LANES:]
    s_re, s_im = both[PATCH:, :LANES], both[PATCH:, LANES:]
    if sign < 0:
        return c_re + s_im, c_im - s_re
    return c_re - s_im, c_im + s_re


def power(re, im):
    lane = lax.broadcasted_iota(jnp.int32, (1, LANES), 1)
    total = jnp.sum(re * re + im * im, axis=0, keepdims=True)
    left = jnp.sum(jnp.where(lane < PATCH, total, 0.0), axis=1, keepdims=True)
    right = jnp.sum(jnp.where(lane < PATCH, 0.0, total), axis=1, keepdims=True)
    return jnp.where(lane < PATCH, left, right) * (1.0 / (PATCH * PATCH))


def window_kernel(offsets, *rest, chunks):
    inner_refs, rest = rest[: len(chunks)], rest[len(chunks) :]
    outer_ref, lane_ref, column_ref = rest[:3]
    spec_ref, image = rest[3:]
    lines, pairs = outer_ref.shape[1], outer_ref.shape[2] // LANES - 1
    lane = lax.broadcasted_iota(jnp.int32, (1, LANES), 1)
    edge = jnp.zeros((HALF, image.shape[2]), F32)
    for part in range(2):
        image[part, :HALF, :] = edge
        image[part, HALF + lines : 2 * HALF + lines, :] = edge
    where = [(c, t) for c, tiles in enumerate(chunks) for t in range(tiles)]
    for u in range(pairs + 1):
        for part in range(2):
            fresh = outer_ref[part, :, u * LANES : (u + 1) * LANES].astype(F32)
            at = slice(HALF, HALF + lines)
            if u == pairs:
                image[part, at, 2 * u * LANES : (2 * u + 1) * LANES] = fresh
                continue
            c, t = where[u]
            known = inner_refs[c][part, :, t * LANES : (t + 1) * LANES].astype(F32)
            image[part, at, 2 * u * LANES : (2 * u + 1) * LANES] = jnp.where(
                lane < 64, fresh, pltpu.roll(known, 64, 1)
            )
            image[part, at, (2 * u + 1) * LANES : (2 * u + 2) * LANES] = jnp.where(
                lane < 64, pltpu.roll(fresh, 64, 1), known
            )
    row_blocks = lines // (2 * PATCH)
    wide = lax.broadcasted_iota(jnp.int32, (PATCH + 8, LANES), 1)

    def block(i, carry):
        gains, windows = [], []
        for u in range(pairs):
            found = [[], []]
            for side in range(2):
                j = 2 * u + side
                start = 2 * PATCH * i + PATCH + offsets[0, i, j]
                shift = PATCH + offsets[1, i, j]
                back = jnp.bitwise_and(2 * LANES - shift + side * PATCH, LANES - 1)
                base = pl.multiple_of(lax.shift_left(lax.shift_right_logical(start, 3), 3), 8)
                up = PATCH + 8 - jnp.bitwise_and(start, 7)
                for part in range(2):
                    left = image[part, pl.ds(base, PATCH + 8), j * LANES : (j + 1) * LANES]
                    right = image[part, pl.ds(base, PATCH + 8), (j + 1) * LANES : (j + 2) * LANES]
                    turned = pltpu.roll(jnp.where(wide >= shift, left, right), back, 1)
                    found[part].append(pltpu.roll(turned, up, 0)[:PATCH])
            re = jnp.where(lane < PATCH, found[0][0], found[0][1])
            im = jnp.where(lane < PATCH, found[1][0], found[1][1])
            gains.append(lax.rsqrt(power(re, im) + EPS) * (1.0 / PATCH**3))
            windows.append(jnp.concatenate([re, im], axis=1))
        stack = jnp.concatenate(windows, axis=0).astype(BF16)
        mixed = dot(stack, lane_ref[0]) + dot(stack, lane_ref[1])
        for u in range(pairs):
            re, im = columns(mixed[u * PATCH : (u + 1) * PATCH], column_ref, -1)
            spec_ref[0, i * pairs + u] = re * gains[u]
            spec_ref[1, i * pairs + u] = im * gains[u]
        return carry

    lax.fori_loop(0, row_blocks, block, 0, unroll=True)


def window_spectra(inner, outer, patch, offsets, chunks):
    lines, pairs = outer.shape[1], outer.shape[2] // LANES - 1
    vmem = pl.BlockSpec(memory_space=pltpu.VMEM)
    return pl.pallas_call(
        functools.partial(window_kernel, chunks=chunks),
        in_specs=[pl.BlockSpec(memory_space=pltpu.SMEM)] + [vmem] * (len(chunks) + 3),
        out_specs=vmem,
        out_shape=jax.ShapeDtypeStruct((2, lines // (2 * PATCH) * pairs, PATCH, LANES), F32),
        scratch_shapes=[
            pltpu.VMEM((2, lines + 2 * HALF + 8, (2 * pairs + 1) * LANES), F32),
        ],
        compiler_params=pltpu.CompilerParams(vmem_limit_bytes=VMEM_BYTES),
        cost_estimate=cost(4.0),
        name="window_spectra",
    )(offsets, *inner, outer, patch[0], patch[2])


def primary_kernel(reference, *rest, parts):
    shares, (lane_ref, column_ref, out_ref, scr) = rest[:-4], rest[-4:]
    source = lax.axis_index("acq") ^ reference[0] if parts > 1 else 0
    for k in range(parts):

        @pl.when(source == k)
        def _(k=k):
            col = 0
            for ref in shares[k::parts]:
                scr[:, :, col : col + ref.shape[2]] = ref[...]
                col += ref.shape[2]

    rows, cols = scr.shape[1], scr.shape[2]
    for u in range(cols // LANES):
        lanes = slice(u * LANES, (u + 1) * LANES)
        both = jnp.concatenate([scr[0, :, lanes], scr[1, :, lanes]], axis=1)
        mixed = dot(both, lane_ref[0]) + dot(both, lane_ref[1])
        for i in range(rows // PATCH):
            at = slice(i * PATCH, (i + 1) * PATCH)
            value = both[at].astype(F32)
            gain = lax.rsqrt(power(value[:, :LANES], value[:, LANES:]) + EPS)
            re, im = columns(mixed[at], column_ref, -1)
            out_ref[0, at, lanes] = (re * gain).astype(BF16)
            out_ref[1, at, lanes] = (im * gain).astype(BF16)


def primary_spectra(reference, shares, patch):
    vmem = pl.BlockSpec(memory_space=pltpu.VMEM)
    flat = [share for chunk in shares for share in chunk]
    shape = flat[0].shape[:2] + (sum(chunk[0].shape[2] for chunk in shares),)
    return pl.pallas_call(
        functools.partial(primary_kernel, parts=len(shares[0])),
        in_specs=[pl.BlockSpec(memory_space=pltpu.SMEM)] + [vmem] * (len(flat) + 2),
        out_specs=vmem,
        out_shape=jax.ShapeDtypeStruct(shape, BF16),
        scratch_shapes=[pltpu.VMEM(shape, BF16)],
        compiler_params=pltpu.CompilerParams(vmem_limit_bytes=VMEM_BYTES),
        cost_estimate=cost(1.0),
        name="primary_spectra",
    )(reference, *flat, patch[0], patch[2])


def correlate_kernel(*rest, parts):
    shares, (spec_ref, inverse_ref, column_ref, out_ref) = rest[:parts], rest[parts:]
    _, rows, cols = shares[0].shape
    pairs = cols // LANES
    per = rows // PATCH
    me = lax.axis_index("acq") if parts > 1 else 0
    for k in range(parts):
        for r in range(per):
            i = (me ^ k) * per + r
            middle = []
            for u in range(pairs):
                at, lanes = slice(r * PATCH, (r + 1) * PATCH), slice(u * LANES, (u + 1) * LANES)
                p_re, p_im = shares[k][0, at, lanes].astype(F32), shares[k][1, at, lanes].astype(F32)
                s_re, s_im = spec_ref[0, i * pairs + u], spec_ref[1, i * pairs + u]
                cross = jnp.concatenate([p_re * s_re + p_im * s_im, p_im * s_re - p_re * s_im], axis=1)
                middle.append(jnp.concatenate(columns(cross, column_ref, 1), axis=1))
            surface = three_pass(split(jnp.concatenate(middle, axis=0)), inverse_ref[0], inverse_ref[1])
            line = pl.ds(pl.multiple_of(i * PATCH, PATCH), PATCH)
            for u in range(pairs):
                lanes = slice(u * LANES, (u + 1) * LANES)
                block = surface[u * PATCH : (u + 1) * PATCH]
                out_ref[0, 0, line, lanes] = block[:, :LANES]
                out_ref[0, 1, line, lanes] = block[:, LANES:]


def correlate(shares, spectrum, patch):
    parts = len(shares)
    _, rows, cols = shares[0].shape
    vmem = pl.BlockSpec(memory_space=pltpu.VMEM)
    return pl.pallas_call(
        functools.partial(correlate_kernel, parts=parts),
        in_specs=[vmem] * (parts + 3),
        out_specs=vmem,
        out_shape=jax.ShapeDtypeStruct((1, 2, rows * parts, cols), F32),
        compiler_params=pltpu.CompilerParams(vmem_limit_bytes=VMEM_BYTES),
        cost_estimate=cost(2.0),
        name="correlate",
    )(*shares, spectrum, patch[1], patch[2])


def far_first(devices):
    return list(range(2, devices)) + list(range(min(2, devices)))[::-1]


def trade(block, k, axis):
    if k == 0:
        return block
    return lax.ppermute(block, axis, [(i, i ^ k) for i in range(lax.axis_size(axis))])


def on_device(echo, filt, slope, centre, valid, reference, offsets):
    devices, parts = lax.axis_size("lines"), lax.axis_size("acq")
    rows, length = echo.shape[2], echo.shape[3]
    lines = rows * devices
    tiles = length // devices // (2 * LANES)
    chunks = (tiles // COLUMN_PARTS,) * COLUMN_PARTS if tiles % COLUMN_PARTS == 0 else (tiles,)
    row_parts = ROW_PARTS if rows % (32 * ROW_PARTS) == 0 else 1
    spread = lines // (2 * PATCH) % parts == 0
    matrices = azimuth_matrices(lines)
    patch = patch_matrices()
    inner = [[[] for _ in range(devices)] for _ in chunks]
    outer = []
    for h in range(row_parts):
        mine, outer = compress(echo[0], filt[0], slope, centre, valid, devices, h, row_parts, chunks, outer)
        for c in range(len(chunks)):
            for k in far_first(devices):
                inner[c][k].append(trade(mine[k][c], k, "lines"))
    near = trade(outer[1], 1, "lines")
    if len(inner) > 1:
        inner[-1], near = lax.optimization_barrier((inner[-1], near))
    images, primaries = [], []
    for c in range(len(chunks)):
        image, *shares = focus_inner(
            inner[c], slope, centre, matrices, 2 * sum(chunks[:c]), parts if spread else 1
        )
        images.append(image)
        if spread:
            shares = {k: trade(shares[k], k, "acq") for k in far_first(parts)}
            shares = [shares[k] for k in range(parts)]
        else:
            mine = lax.axis_index("acq") == reference[0]
            shares = [lax.psum(jnp.where(mine, shares[0], 0).astype(BF16), "acq")]
        primaries.append(shares)
    far, _ = lax.optimization_barrier((list(outer[2:]), images[0]))
    far = [trade(block, k + 2, "lines") for k, block in enumerate(far)]
    outer = [outer[0], near, *far]
    outer = focus_outer(outer, slope, centre, matrices)
    spectrum = window_spectra(images, outer, patch, offsets[0], chunks)
    shares = [primary_spectra(reference, primaries, patch)]
    for k in range(1, parts if spread else 1):
        low = k & -k
        shares.append(trade(shares[k - low], low, "acq"))
    return correlate(shares, spectrum, patch)


def solution(mesh):
    return jax.shard_map(
        on_device,
        mesh=mesh,
        in_specs=(
            P(("stack", "acq"), None, "lines", None),
            P(("stack", "acq"), None, None),
            P(("stack", "acq"), "lines"),
            P(("stack", "acq"), "lines"),
            P(("stack", "acq")),
            P("stack"),
            P(("stack", "acq"), None, None, "lines"),
        ),
        out_specs=P(("stack", "acq"), None, None, "lines"),
        check_vma=False,
    )
```
